32 devices in a mesh: gx: 4 (over x, core), gy: 8 (over z, y).
Axes of the slice: x: 2, y: 2, z: 4, core: 2. Of those that a mesh axis runs over, the one named last changes fastest.
Arguments:
- positions: float32 [3, 4, 8, 128], P(None, 'gx', 'gy'), may hold values from 0 to 20
- spring: float32 [4, 8, 128], P('gx', 'gy'), may hold values from 0.25 to 4
- border: int32 [4, 8, 32], P('gx', 'gy'), may hold values from 0 to 127, as said below
- neighbours: int32 [4, 8, 64, 128], P('gx', 'gy'), may hold values from -1 to 1055, as said below
- vec_prev: float32 [3, 8, 4, 8, 128], P(None, None, 'gx', 'gy'), may hold values from -6 to 6
- vec_now: float32 [3, 8, 4, 8, 128], P(None, None, 'gx', 'gy'), may hold values from -6 to 6
- heat_prev: float32 [3, 8, 4, 8, 128], P(None, None, 'gx', 'gy'), may hold values from -6 to 6
- heat_now: float32 [3, 8, 4, 8, 128], P(None, None, 'gx', 'gy'), may hold values from -6 to 6
Outputs:
- vec_next: float32 [3, 8, 4, 8, 128], P(None, None, 'gx', 'gy')
- vec_after: float32 [3, 8, 4, 8, 128], P(None, None, 'gx', 'gy')
- heat_next: float32 [3, 8, 4, 8, 128], P(None, None, 'gx', 'gy')
- heat_after: float32 [3, 8, 4, 8, 128], P(None, None, 'gx', 'gy')
The draws below stay inside these ranges and needn't reach their ends.
Inputs may be any that keep to these rules, and one draw needn't show every extreme that they name: `border`: each column's row lists 32 different atoms of that column. `neighbours`: -1 marks an empty slot, and empty slots follow the used ones; an entry o * 128 + k names for o = 4 the column's own atom k, else entry k (k < 32) of the border table of the column o // 3 - 1 steps along x and o % 3 - 1 steps along y (periodic); every atom uses at least 32 slots and some atom of every column uses all 64.
All inputs are finite; a program needn't handle non-finite values.
Results may differ from the reference program's by a relative error of at most 0.0003.
Values sent between devices are 32-bit elements; how exact they have to be, the bound alone decides.
A program may use at most 64 MiB of HBM per device.

```python
import math
import jax
import jax.numpy as jnp
from jax import lax

A = 128
R = 8
NB = 64
G = 32
COLS_X = 4
COLS_Y = 8


def draw_border(key, part):
    keys = jax.random.split(jax.random.fold_in(key, 5), COLS_X * COLS_Y)
    chosen_rows = jax.vmap(lambda k: jax.random.permutation(k, A)[:G])(keys)
    return chosen_rows.reshape(COLS_X, COLS_Y, G).astype(jnp.int32)


def draw_neighbours(key, part):
    keys = jax.random.split(jax.random.fold_in(key, 11), 5)
    shape = (COLS_X, COLS_Y, NB, A)
    picked = jax.random.randint(keys[0], shape, 0, 16)
    offset = jnp.where(picked >= 9, 4, picked)
    own_atom = jax.random.randint(keys[1], shape, 0, A)
    border_slot = jax.random.randint(keys[2], shape, 0, G)
    within = jnp.where(offset == 4, own_atom, border_slot)
    counts = jax.random.randint(keys[3], (COLS_X, COLS_Y, 1, A), NB // 2, NB + 1)
    fullest = jax.random.randint(keys[4], (COLS_X, COLS_Y, 1, 1), 0, A)
    counts = jnp.where(jnp.arange(A)[None, None, None, :] == fullest, NB, counts)
    live = jnp.arange(NB)[None, None, :, None] < counts
    return jnp.where(live, offset * A + within, -1).astype(jnp.int32)


def shard_levels(rng, extent, pieces, low, largest):
    def one(dim, parts):
        heights = jax.random.uniform(jax.random.fold_in(jax.random.fold_in(rng, 6), dim), (parts,), jnp.float32, low / len(pieces), largest / len(pieces))
        return jnp.repeat(jnp.exp(heights), extent[dim] // parts).reshape((-1,) + (1,) * (len(extent) - dim - 1))

    factor_of = one(*pieces[0])
    for cut in pieces[1:]:
        factor_of = factor_of * one(*cut)
    return factor_of


def noise(rng, extent, deviation, reach, cuts=(), kind=jnp.bfloat16):
    loudness = shard_levels(rng, extent, cuts, -0.22, 0.18) if cuts else 1.0
    values = jax.random.normal(rng, extent, jnp.float32) * deviation * loudness
    return jnp.minimum(jnp.maximum(values, -reach), reach).astype(kind)


def setup_inputs(seed: int = 0) -> dict:
    arg_keys = jax.random.split(jax.random.key(seed), 9)
    positions = jnp.clip(20.0 * jax.random.uniform(arg_keys[0], (3, COLS_X, COLS_Y, A), jnp.float32) ** shard_levels(arg_keys[0], (3, COLS_X, COLS_Y, A), ((1, 4), (2, 8)), -0.2, 0.2), 0.0, 20.0)
    spring = jnp.clip(jnp.exp(math.log(4.0) - 2.7725887 * jax.random.uniform(arg_keys[1], (COLS_X, COLS_Y, A), jnp.float32) ** shard_levels(arg_keys[1], (COLS_X, COLS_Y, A), ((0, 4), (1, 8)), -0.2, 0.2)), 0.25, 4.0)
    border = draw_border(jax.random.fold_in(arg_keys[8], 71), 0)
    neighbours = draw_neighbours(jax.random.fold_in(arg_keys[8], 71), 0)
    vec_prev = noise(arg_keys[4], (3, R, COLS_X, COLS_Y, A), 1.0, 6.0, ((2, 4), (3, 8)), jnp.float32)
    vec_now = noise(arg_keys[5], (3, R, COLS_X, COLS_Y, A), 1.0, 6.0, ((2, 4), (3, 8)), jnp.float32)
    heat_prev = noise(arg_keys[6], (3, R, COLS_X, COLS_Y, A), 1.0, 6.0, ((2, 4), (3, 8)), jnp.float32)
    heat_now = noise(arg_keys[7], (3, R, COLS_X, COLS_Y, A), 1.0, 6.0, ((2, 4), (3, 8)), jnp.float32)
    return dict(positions=positions, spring=spring, border=border, neighbours=neighbours, vec_prev=vec_prev, vec_now=vec_now, heat_prev=heat_prev, heat_now=heat_now)


column_edge = 20.0
reach_sq = 64.0

def reference(positions, spring, border, neighbours, vec_prev, vec_now, heat_prev, heat_now):
    cols_x, cols_y, n_atoms = spring.shape
    n_slots = neighbours.shape[2]
    n_border = border.shape[-1]
    n_vec = vec_prev.shape[1]
    flat_pos = positions.reshape(3, -1)
    flat_spring = spring.reshape(-1)
    flat_border = border.reshape(-1)
    grid_x = jnp.arange(cols_x, dtype=jnp.int32)[:, None, None]
    grid_y = jnp.arange(cols_y, dtype=jnp.int32)[None, :, None]
    slot_major = jnp.moveaxis(neighbours, 2, 0)

    def operate_on(current):
        n_rows = current.shape[1]
        flat_cur = current.reshape(3, n_rows, -1)

        def slot_step(total, entries):
            usable = entries >= 0
            entry_safe = jnp.maximum(entries, 0)
            offset = entry_safe // n_atoms
            within = entry_safe % n_atoms
            step_x = offset // 3 - 1
            step_y = offset % 3 - 1
            column = (grid_x + step_x) % cols_x * cols_y + (grid_y + step_y) % cols_y
            lookup = jnp.take(flat_border, column * n_border + jnp.minimum(within, n_border - 1))
            atom = jnp.where(offset == 4, within, lookup)
            flat = (column * n_atoms + atom).reshape(-1).astype(jnp.int32)
            far_pos = flat_pos[:, flat].reshape(3, cols_x, cols_y, n_atoms)
            far_spring = flat_spring[flat].reshape(cols_x, cols_y, n_atoms)
            delta_x = far_pos[0] + step_x.astype(jnp.float32) * column_edge - positions[0]
            delta_y = far_pos[1] + step_y.astype(jnp.float32) * column_edge - positions[1]
            delta_z = far_pos[2] - positions[2]
            dist_sq = delta_x * delta_x + delta_y * delta_y + delta_z * delta_z
            coupling = jnp.where(usable, jnp.sqrt(spring * far_spring) / (n_slots * (1.0 + dist_sq / reach_sq)), jnp.float32(0.0))
            bending = 2.0 / (dist_sq + 1.0)
            far_rows = flat_cur[:, :, flat].reshape(3, n_rows, cols_x, cols_y, n_atoms)
            u = current - far_rows
            proj = delta_x * u[0] + delta_y * u[1] + delta_z * u[2]
            displace = jnp.stack([delta_x, delta_y, delta_z])[:, None]
            contrib = coupling * (u + bending * displace * proj[None])
            return (total + contrib, None)
        total, _ = lax.scan(slot_step, jnp.zeros_like(current), slot_major)
        return total - current
    state_zero = jnp.concatenate([vec_prev, heat_prev], axis=1)
    state_one = jnp.concatenate([vec_now, heat_now], axis=1)
    state_two = 2.0 * operate_on(state_one) - state_zero
    state_three = 2.0 * operate_on(state_two) - state_one
    return (state_two[:, :n_vec], state_three[:, :n_vec], state_two[:, n_vec:], state_three[:, n_vec:])
```

```python
import functools

import jax
import jax.numpy as jnp
from jax import lax
from jax.experimental import pallas as pl
from jax.experimental.pallas import tpu as pltpu
from jax.sharding import PartitionSpec as P

column_edge = 20.0
reach_sq = 64.0
MESH = pl.DeviceIdType.MESH
offsets = (0, 1, 2, 3, 5, 6, 7, 8)
pairs = ((0, 0), (0, 1), (1, 1), (1, 2), (2, 2), (0, 2))


def halves(values):
    high = values.astype(jnp.bfloat16)
    return high, (values - high.astype(jnp.float32)).astype(jnp.bfloat16)


def kernel(
    count_x, count_y,
    pos_ref, spring_ref, border_ref, nbr_ref, vp_ref, vn_ref, hp_ref, hn_ref,
    vec_next, vec_after, heat_next, heat_after,
    out_buf, in_buf, key_buf, amount_buf, times_buf, mat_hi, mat_lo, send_sem, recv_sem,
):
    n_slots, n_atoms = nbr_ref.shape
    n_border = border_ref.shape[1]
    groups = n_atoms // n_border
    n_vec = vp_ref.shape[0] // 3
    n_rows = 2 * n_vec
    gx, gy = lax.axis_index("gx"), lax.axis_index("gy")

    def device(rank):
        dx, dy = offsets[rank] // 3 - 1, offsets[rank] % 3 - 1
        return lax.rem(gx + dx + count_x, count_x), lax.rem(gy + dy + count_y, count_y)

    barrier = pltpu.get_barrier_semaphore()
    for rank in range(8):
        pl.semaphore_signal(barrier, inc=1, device_id=device(rank), device_id_type=MESH)

    lane_group = lax.broadcasted_iota(jnp.int32, (n_rows, n_atoms), 1) // n_border
    chosen = jnp.concatenate([border_ref[...]] * groups, axis=1)
    chosen = jnp.broadcast_to(chosen, (n_rows, n_atoms))

    def copies(turn):
        return [
            pltpu.make_async_remote_copy(
                src_ref=out_buf.at[turn, (7 - rank) % 4],
                dst_ref=in_buf.at[turn, 7 - rank],
                send_sem=send_sem.at[turn, rank],
                recv_sem=recv_sem.at[turn, 7 - rank],
                device_id=device(rank),
                device_id_type=MESH,
            )
            for rank in range(8)
        ]

    def pack(turn, parts):
        taken = [jnp.take_along_axis(part, chosen, axis=1) for part in parts]
        for k in range(4):
            mixed = taken[0]
            for s in range(1, len(taken)):
                mixed = jnp.where(lane_group == (s + k) % 4, taken[s], mixed)
            out_buf[turn, k] = mixed

    def unpack(turn, s):
        tiles = []
        for half in range(2):
            mixed = in_buf[turn, 4 * half + (0 - s) % 4]
            for g in range(1, 4):
                mixed = jnp.where(lane_group == g, in_buf[turn, 4 * half + (g - s) % 4], mixed)
            tiles.append(pltpu.roll(mixed, (n_atoms - n_border * s) % n_atoms, 1) if s else mixed)
        return jnp.concatenate(tiles, axis=1)

    def fields(vec, heat):
        return [
            jnp.concatenate(
                [vec[a * n_vec : (a + 1) * n_vec], heat[a * n_vec : (a + 1) * n_vec]], axis=0
            )
            for a in range(3)
        ]

    own_pos = pos_ref[...]
    root = jnp.sqrt(spring_ref[...])
    geometry = jnp.concatenate(
        [own_pos, root, jnp.zeros((n_rows - 4, n_atoms), jnp.float32)], axis=0
    )
    state_one = fields(vn_ref[...], hn_ref[...])
    pack(0, state_one + [geometry])

    pl.semaphore_wait(barrier, 8)
    first = copies(0)
    for copy in first:
        copy.start()

    entries = nbr_ref[...]
    shift = n_atoms.bit_length() - 1
    small = n_border.bit_length() - 1
    offset = entries >> shift
    within = entries & (n_atoms - 1)
    block = jnp.where(
        offset == 4, within >> small, jnp.where(offset > 4, offset + groups - 1, offset + groups)
    )
    word = (block >> 2) * n_border + (within & (n_border - 1))
    key_buf[...] = jnp.where(entries < 0, -1, word)
    amount_buf[...] = jnp.left_shift(jnp.int32(1), (block & 3) * 8)
    n_words = 3 * n_border
    numbers = lax.broadcasted_iota(jnp.int32, (n_words, n_atoms), 0)

    def add_slots(turn, total):
        start = pl.multiple_of(turn * 8, 8)
        keys = key_buf[pl.ds(start, 8), :]
        amounts = amount_buf[pl.ds(start, 8), :]
        for n in range(8):
            total = total + jnp.where(numbers == keys[n : n + 1], amounts[n : n + 1], 0)
        return total

    words = lax.fori_loop(
        0, n_slots // 8, add_slots, jnp.zeros((n_words, n_atoms), jnp.int32)
    )
    for g in range(3):
        for f in range(4):
            row = (4 * g + f) * n_border
            part = words[g * n_border : (g + 1) * n_border]
            times_buf[row : row + n_border] = ((part >> (8 * f)) & 255).astype(jnp.float32)

    def build(row, columns, sums):
        delta = [columns[:, a : a + 1] - own_pos[a : a + 1] for a in range(3)]
        dist_sq = delta[0] * delta[0] + delta[1] * delta[1] + delta[2] * delta[2]
        scale = times_buf[row : row + n_border] * (columns[:, 3:4] * root)
        near = dist_sq + 1.0
        share = scale / (near * (n_slots + dist_sq * (n_slots / reach_sq)))
        coupling = share * near
        bent = [(share + share) * part for part in delta]
        out = []
        for index, (a, b) in enumerate(pairs):
            entry = bent[a] * delta[b]
            if a == b:
                entry = entry + coupling
            high, low = halves(entry)
            lanes = slice(index * n_atoms, (index + 1) * n_atoms)
            mat_hi[row : row + n_border, lanes] = high
            mat_lo[row : row + n_border, lanes] = low
            out.append(sums[index] + jnp.sum(entry.reshape(-1, 8, n_atoms), axis=0))
        return out

    def product(rows, sources):
        high, low = halves(jnp.concatenate(sources, axis=0))
        both = jnp.concatenate([high, low], axis=0)
        big = jnp.dot(both, mat_hi[rows, :], preferred_element_type=jnp.float32)
        rest = jnp.dot(high, mat_lo[rows, :], preferred_element_type=jnp.float32)
        return big[: 3 * n_rows] + big[3 * n_rows :] + rest

    def pieces(full):
        return [
            [
                full[b * n_rows : (b + 1) * n_rows, index * n_atoms : (index + 1) * n_atoms]
                for index in range(6)
            ]
            for b in range(3)
        ]

    def gathered(full):
        part = pieces(full)
        place = {pair: index for index, pair in enumerate(pairs)}
        return [
            sum(part[b][place[(min(a, b), max(a, b))]] for b in range(3)) for a in range(3)
        ]

    sums = [jnp.zeros((8, n_atoms), jnp.float32) for _ in pairs]
    columns = jnp.transpose(geometry[:8])
    for g in range(groups):
        sums = build(g * n_border, columns[g * n_border : (g + 1) * n_border], sums)
    home = slice(0, n_atoms)
    away = slice(n_atoms, 3 * n_atoms)
    near_part = product(home, state_one)

    for copy in first:
        copy.wait_recv()
    far_geometry = unpack(0, 3)[:8]
    rank_of_lane = lax.broadcasted_iota(jnp.int32, (1, 2 * n_atoms), 1) // n_border
    offset_of_lane = jnp.where(rank_of_lane >= 4, rank_of_lane + 1, rank_of_lane)
    step_x = offset_of_lane // 3 - 1
    step_y = offset_of_lane - 3 * (step_x + 1) - 1
    far_geometry = jnp.concatenate(
        [
            far_geometry[0:1] + step_x.astype(jnp.float32) * column_edge,
            far_geometry[1:2] + step_y.astype(jnp.float32) * column_edge,
            far_geometry[2:8],
        ],
        axis=0,
    )
    far_columns = jnp.transpose(far_geometry)
    for g in range(8):
        sums = build(
            n_atoms + g * n_border, far_columns[g * n_border : (g + 1) * n_border], sums
        )
    totals = [jnp.sum(part, axis=0, keepdims=True) for part in sums]
    weight = {pair: total for pair, total in zip(pairs, totals)}

    def stepped(state, before, far):
        out = []
        for a in range(3):
            value = sum(weight[(min(a, b), max(a, b))] * state[b] for b in range(3))
            out.append(2.0 * (value - far[a] - state[a]) - before[a])
        return out

    far = gathered(near_part + product(away, [unpack(0, s) for s in range(3)]))
    state_two = stepped(state_one, fields(vp_ref[...], hp_ref[...]), far)
    pack(1, state_two)
    second = copies(1)
    for copy in second:
        copy.start()
    for a in range(3):
        vec_next[a * n_vec : (a + 1) * n_vec] = state_two[a][:n_vec]
        heat_next[a * n_vec : (a + 1) * n_vec] = state_two[a][n_vec:]
    near_part = product(home, state_two)
    for copy in second:
        copy.wait_recv()
    far = gathered(near_part + product(away, [unpack(1, s) for s in range(3)]))
    state_three = stepped(state_two, state_one, far)
    for a in range(3):
        vec_after[a * n_vec : (a + 1) * n_vec] = state_three[a][:n_vec]
        heat_after[a * n_vec : (a + 1) * n_vec] = state_three[a][n_vec:]
    for copy in first + second:
        copy.wait_send()


def shards(positions, spring, border, neighbours, vec_prev, vec_now, heat_prev, heat_now):
    n_atoms = spring.shape[-1]
    n_slots = neighbours.shape[2]
    n_border = border.shape[-1]
    n_vec = vec_prev.shape[1]
    n_rows = 2 * n_vec
    flat = jax.ShapeDtypeStruct((3 * n_vec, n_atoms), jnp.float32)
    vmem = pl.BlockSpec(memory_space=pltpu.VMEM)
    outs = pl.pallas_call(
        functools.partial(kernel, lax.axis_size("gx"), lax.axis_size("gy")),
        out_shape=(flat,) * 4,
        in_specs=[vmem] * 8,
        out_specs=(vmem,) * 4,
        scratch_shapes=[
            pltpu.VMEM((2, 4, n_rows, n_atoms), jnp.float32),
            pltpu.VMEM((2, 8, n_rows, n_atoms), jnp.float32),
            pltpu.VMEM((n_slots, n_atoms), jnp.int32),
            pltpu.VMEM((n_slots, n_atoms), jnp.int32),
            pltpu.VMEM((3 * n_atoms, n_atoms), jnp.float32),
            pltpu.VMEM((3 * n_atoms, 6 * n_atoms), jnp.bfloat16),
            pltpu.VMEM((3 * n_atoms, 6 * n_atoms), jnp.bfloat16),
            pltpu.SemaphoreType.DMA((2, 8)),
            pltpu.SemaphoreType.DMA((2, 8)),
        ],
        compiler_params=pltpu.CompilerParams(
            collective_id=0, has_side_effects=True, vmem_limit_bytes=24 * 1024 * 1024
        ),
        name="chebyshev",
    )(
        positions.reshape(3, n_atoms),
        spring.reshape(1, n_atoms),
        border.reshape(1, n_border),
        neighbours.reshape(n_slots, n_atoms),
        *(x.reshape(3 * n_vec, n_atoms) for x in (vec_prev, vec_now, heat_prev, heat_now)),
    )
    return tuple(out.reshape(vec_prev.shape) for out in outs)


def solution(mesh):
    fields = P(None, None, "gx", "gy", None)
    return jax.shard_map(
        shards,
        mesh=mesh,
        in_specs=(
            P(None, "gx", "gy", None),
            P("gx", "gy", None),
            P("gx", "gy", None),
            P("gx", "gy", None, None),
            fields,
            fields,
            fields,
            fields,
        ),
        out_specs=(fields,) * 4,
        check_vma=False,
    )
```

```python
import functools

import jax
import jax.numpy as jnp
from jax import lax
from jax.experimental import pallas as pl
from jax.experimental.pallas import tpu as pltpu
from jax.sharding import PartitionSpec as P

column_edge = 20.0
reach_sq = 64.0
MESH = pl.DeviceIdType.MESH
offsets = (0, 1, 2, 3, 5, 6, 7, 8)
pairs = ((0, 0), (0, 1), (1, 1), (1, 2), (2, 2), (0, 2))


def halves(values):
    high = values.astype(jnp.bfloat16)
    return high, (values - high.astype(jnp.float32)).astype(jnp.bfloat16)


def kernel(
    count_x, count_y,
    pos_hbm, spring_hbm, border_hbm, nbr_hbm, vp_hbm, vn_hbm, hp_hbm, hn_hbm,
    vec_next, vec_after, heat_next, heat_after,
    geo_buf, border_ref, nbr_ref, field_buf, out_buf, in_buf, key_buf, amount_buf, times_buf,
    column_buf, mat_hi, mat_lo, load_sem, send_sem, recv_sem,
):
    n_slots, n_atoms = nbr_ref.shape
    n_border = border_ref.shape[1]
    groups = n_atoms // n_border
    n_vec = field_buf.shape[1] // 3
    n_rows = 2 * n_vec
    gx, gy = lax.axis_index("gx"), lax.axis_index("gy")

    def device(rank):
        dx, dy = offsets[rank] // 3 - 1, offsets[rank] % 3 - 1
        return lax.rem(gx + dx + count_x, count_x), lax.rem(gy + dy + count_y, count_y)

    barrier = pltpu.get_barrier_semaphore()
    for rank in range(8):
        pl.semaphore_signal(barrier, inc=1, device_id=device(rank), device_id_type=MESH)

    geo_buf[...] = jnp.zeros_like(geo_buf)
    moves = (
        (border_hbm, border_ref),
        (vn_hbm, field_buf.at[0]),
        (hn_hbm, field_buf.at[1]),
        (pos_hbm.at[0], geo_buf.at[0:1]),
        (pos_hbm.at[1], geo_buf.at[1:2]),
        (pos_hbm.at[2], geo_buf.at[2:3]),
        (spring_hbm, geo_buf.at[3:4]),
        (nbr_hbm, nbr_ref),
        (vp_hbm, field_buf.at[2]),
        (hp_hbm, field_buf.at[3]),
    )
    loads = [
        pltpu.make_async_copy(src, dst, load_sem.at[i]) for i, (src, dst) in enumerate(moves)
    ]
    for load in loads:
        load.start()
    for load in loads[:7]:
        load.wait()

    lane_group = lax.broadcasted_iota(jnp.int32, (n_rows, n_atoms), 1) // n_border
    chosen = jnp.concatenate([border_ref[...]] * groups, axis=1)
    chosen = jnp.broadcast_to(chosen, (n_rows, n_atoms))

    def copies(turn):
        return [
            pltpu.make_async_remote_copy(
                src_ref=out_buf.at[turn, (7 - rank) % 4],
                dst_ref=in_buf.at[turn, 7 - rank],
                send_sem=send_sem.at[turn, rank],
                recv_sem=recv_sem.at[turn, 7 - rank],
                device_id=device(rank),
                device_id_type=MESH,
            )
            for rank in range(8)
        ]

    def pack(turn, parts):
        taken = [jnp.take_along_axis(part, chosen, axis=1) for part in parts]
        for k in range(4):
            mixed = taken[0]
            for s in range(1, len(taken)):
                mixed = jnp.where(lane_group == (s + k) % 4, taken[s], mixed)
            out_buf[turn, k] = mixed

    def unpack(turn, s):
        tiles = []
        for half in range(2):
            mixed = in_buf[turn, 4 * half + (0 - s) % 4]
            for g in range(1, 4):
                mixed = jnp.where(lane_group == g, in_buf[turn, 4 * half + (g - s) % 4], mixed)
            tiles.append(pltpu.roll(mixed, (n_atoms - n_border * s) % n_atoms, 1) if s else mixed)
        return jnp.concatenate(tiles, axis=1)

    def fields(vec, heat):
        return [
            jnp.concatenate(
                [vec[a * n_vec : (a + 1) * n_vec], heat[a * n_vec : (a + 1) * n_vec]], axis=0
            )
            for a in range(3)
        ]

    geometry = geo_buf[...]
    row_of = lax.broadcasted_iota(jnp.int32, geometry.shape, 0)
    geometry = jnp.where(row_of == 3, jnp.sqrt(geometry), geometry)
    own_pos = geometry[0:3]
    root = geometry[3:4]
    state_one = fields(field_buf[0], field_buf[1])
    pack(0, state_one + [geometry])

    loads[7].wait()
    entries = nbr_ref[...]
    shift = n_atoms.bit_length() - 1
    small = n_border.bit_length() - 1
    offset = entries >> shift
    within = entries & (n_atoms - 1)
    block = jnp.where(
        offset == 4, within >> small, jnp.where(offset > 4, offset + groups - 1, offset + groups)
    )
    word = (block >> 2) * n_border + (within & (n_border - 1))
    key_buf[...] = jnp.where(entries < 0, -1, word)
    amount_buf[...] = jnp.left_shift(jnp.int32(1), (block & 3) * 8)
    n_words = 3 * n_border
    numbers = lax.broadcasted_iota(jnp.int32, (n_words, n_atoms), 0)

    def add_slots(turn, total):
        start = pl.multiple_of(turn * 8, 8)
        keys = key_buf[pl.ds(start, 8), :]
        amounts = amount_buf[pl.ds(start, 8), :]
        for n in range(8):
            total = total + jnp.where(numbers == keys[n : n + 1], amounts[n : n + 1], 0)
        return total

    words = lax.fori_loop(
        0, n_slots // 8, add_slots, jnp.zeros((n_words, n_atoms), jnp.int32)
    )
    for g in range(3):
        for f in range(4):
            row = (4 * g + f) * n_border
            part = words[g * n_border : (g + 1) * n_border]
            times_buf[row : row + n_border] = ((part >> (8 * f)) & 255).astype(jnp.float32)

    pl.semaphore_wait(barrier, 8)
    first = copies(0)
    for copy in first:
        copy.start()

    def build(turn, sums):
        group = pl.ds(pl.multiple_of(turn * n_border, n_border), n_border)
        columns = column_buf[group, :]
        delta = [columns[:, a : a + 1] - own_pos[a : a + 1] for a in range(3)]
        dist_sq = delta[0] * delta[0] + delta[1] * delta[1] + delta[2] * delta[2]
        scale = times_buf[group, :] * (columns[:, 3:4] * root)
        near = dist_sq + 1.0
        share = scale / (near * (n_slots + dist_sq * (n_slots / reach_sq)))
        coupling = share * near
        bent = [(share + share) * part for part in delta]
        out = []
        for index, (a, b) in enumerate(pairs):
            entry = bent[a] * delta[b]
            if a == b:
                entry = entry + coupling
            high, low = halves(entry)
            lanes = slice(index * n_atoms, (index + 1) * n_atoms)
            mat_hi[group, lanes] = high
            mat_lo[group, lanes] = low
            out.append(sums[index] + jnp.sum(entry.reshape(-1, 8, n_atoms), axis=0))
        return tuple(out)

    def product(rows, sources):
        high, low = halves(jnp.concatenate(sources, axis=0))
        both = jnp.concatenate([high, low], axis=0)
        big = jnp.dot(both, mat_hi[rows, :], preferred_element_type=jnp.float32)
        rest = jnp.dot(high, mat_lo[rows, :], preferred_element_type=jnp.float32)
        return big[: 3 * n_rows] + big[3 * n_rows :] + rest

    def pieces(full):
        return [
            [
                full[b * n_rows : (b + 1) * n_rows, index * n_atoms : (index + 1) * n_atoms]
                for index in range(6)
            ]
            for b in range(3)
        ]

    def gathered(full):
        part = pieces(full)
        place = {pair: index for index, pair in enumerate(pairs)}
        return [
            sum(part[b][place[(min(a, b), max(a, b))]] for b in range(3)) for a in range(3)
        ]

    sums = tuple(jnp.zeros((8, n_atoms), jnp.float32) for _ in pairs)
    column_buf[:n_atoms] = jnp.transpose(geometry[:8])
    sums = lax.fori_loop(0, groups, build, sums)
    home = slice(0, n_atoms)
    away = slice(n_atoms, 3 * n_atoms)
    near_part = product(home, state_one)

    for copy in first:
        copy.wait_recv()
    far_geometry = unpack(0, 3)[:8]
    rank_of_lane = lax.broadcasted_iota(jnp.int32, (1, 2 * n_atoms), 1) // n_border
    offset_of_lane = jnp.where(rank_of_lane >= 4, rank_of_lane + 1, rank_of_lane)
    step_x = offset_of_lane // 3 - 1
    step_y = offset_of_lane - 3 * (step_x + 1) - 1
    far_geometry = jnp.concatenate(
        [
            far_geometry[0:1] + step_x.astype(jnp.float32) * column_edge,
            far_geometry[1:2] + step_y.astype(jnp.float32) * column_edge,
            far_geometry[2:8],
        ],
        axis=0,
    )
    column_buf[n_atoms:] = jnp.transpose(far_geometry)
    sums = lax.fori_loop(groups, groups + 8, build, sums)
    totals = [jnp.sum(part, axis=0, keepdims=True) for part in sums]
    weight = {pair: total for pair, total in zip(pairs, totals)}

    def stepped(state, before, far):
        out = []
        for a in range(3):
            value = sum(weight[(min(a, b), max(a, b))] * state[b] for b in range(3))
            out.append(2.0 * (value - far[a] - state[a]) - before[a])
        return out

    far = gathered(near_part + product(away, [unpack(0, s) for s in range(3)]))
    for load in loads[8:]:
        load.wait()
    state_two = stepped(state_one, fields(field_buf[2], field_buf[3]), far)
    pack(1, state_two)
    second = copies(1)
    for copy in second:
        copy.start()
    for a in range(3):
        vec_next[a * n_vec : (a + 1) * n_vec] = state_two[a][:n_vec]
        heat_next[a * n_vec : (a + 1) * n_vec] = state_two[a][n_vec:]
    near_part = product(home, state_two)
    for copy in second:
        copy.wait_recv()
    far = gathered(near_part + product(away, [unpack(1, s) for s in range(3)]))
    state_three = stepped(state_two, state_one, far)
    for a in range(3):
        vec_after[a * n_vec : (a + 1) * n_vec] = state_three[a][:n_vec]
        heat_after[a * n_vec : (a + 1) * n_vec] = state_three[a][n_vec:]
    for copy in first + second:
        copy.wait_send()


def deliver(*refs):
    sem = refs[8]
    moves = [pltpu.make_async_copy(refs[i], refs[4 + i], sem.at[i]) for i in range(4)]
    for move in moves:
        move.start()
    for move in moves:
        move.wait()


def shards(positions, spring, border, neighbours, vec_prev, vec_now, heat_prev, heat_now):
    n_atoms = spring.shape[-1]
    n_slots = neighbours.shape[2]
    n_border = border.shape[-1]
    n_vec = vec_prev.shape[1]
    n_rows = 2 * n_vec
    flat = jax.ShapeDtypeStruct((3 * n_vec, n_atoms), jnp.float32)
    vmem = pl.BlockSpec(memory_space=pltpu.VMEM)
    hbm = pl.BlockSpec(memory_space=pltpu.HBM)
    made = pl.pallas_call(
        functools.partial(kernel, lax.axis_size("gx"), lax.axis_size("gy")),
        out_shape=(flat,) * 4,
        in_specs=[hbm] * 8,
        out_specs=(vmem,) * 4,
        scratch_shapes=[
            pltpu.VMEM((n_rows, n_atoms), jnp.float32),
            pltpu.VMEM((1, n_border), jnp.int32),
            pltpu.VMEM((n_slots, n_atoms), jnp.int32),
            pltpu.VMEM((4, 3 * n_vec, n_atoms), jnp.float32),
            pltpu.VMEM((2, 4, n_rows, n_atoms), jnp.float32),
            pltpu.VMEM((2, 8, n_rows, n_atoms), jnp.float32),
            pltpu.VMEM((n_slots, n_atoms), jnp.int32),
            pltpu.VMEM((n_slots, n_atoms), jnp.int32),
            pltpu.VMEM((3 * n_atoms, n_atoms), jnp.float32),
            pltpu.VMEM((3 * n_atoms, 8), jnp.float32),
            pltpu.VMEM((3 * n_atoms, 6 * n_atoms), jnp.bfloat16),
            pltpu.VMEM((3 * n_atoms, 6 * n_atoms), jnp.bfloat16),
            pltpu.SemaphoreType.DMA((10,)),
            pltpu.SemaphoreType.DMA((2, 8)),
            pltpu.SemaphoreType.DMA((2, 8)),
        ],
        compiler_params=pltpu.CompilerParams(
            collective_id=0, has_side_effects=True, vmem_limit_bytes=24 * 1024 * 1024
        ),
        name="chebyshev",
    )(
        *(
            pltpu.with_memory_space_constraint(x, pltpu.HBM)
            for x in (
                positions.reshape(3, 1, n_atoms),
                spring.reshape(1, n_atoms),
                border.reshape(1, n_border),
                neighbours.reshape(n_slots, n_atoms),
                *(x.reshape(3 * n_vec, n_atoms) for x in (vec_prev, vec_now, heat_prev, heat_now)),
            )
        ),
    )
    outs = pl.pallas_call(
        deliver,
        out_shape=(flat,) * 4,
        in_specs=[vmem] * 4,
        out_specs=(hbm,) * 4,
        scratch_shapes=[pltpu.SemaphoreType.DMA((4,))],
        name="deliver",
    )(*made)
    return tuple(out.reshape(vec_prev.shape) for out in outs)


def solution(mesh):
    fields = P(None, None, "gx", "gy", None)
    return jax.shard_map(
        shards,
        mesh=mesh,
        in_specs=(
            P(None, "gx", "gy", None),
            P("gx", "gy", None),
            P("gx", "gy", None),
            P("gx", "gy", None, None),
            fields,
            fields,
            fields,
            fields,
        ),
        out_specs=(fields,) * 4,
        check_vma=False,
    )
```

```python
import functools

import jax
import jax.numpy as jnp
from jax import lax
from jax.experimental import pallas as pl
from jax.experimental.pallas import tpu as pltpu
from jax.sharding import PartitionSpec as P

column_edge = 20.0
reach_sq = 64.0
MESH = pl.DeviceIdType.MESH
offsets = (0, 1, 2, 3, 5, 6, 7, 8)
send_order = (0, 3, 5, 2, 4, 7, 1, 6)
pairs = ((0, 0), (0, 1), (1, 1), (1, 2), (2, 2), (0, 2))


def halves(values):
    high = values.astype(jnp.bfloat16)
    return high, (values - high.astype(jnp.float32)).astype(jnp.bfloat16)


def kernel(
    count_x, count_y,
    pos_hbm, spring_hbm, border_hbm, nbr_hbm, vp_hbm, vn_hbm, hp_hbm, hn_hbm,
    vec_next, vec_after, heat_next, heat_after,
    geo_buf, border_ref, nbr_ref, field_buf, out_buf, in_buf, key_buf, amount_buf, times_buf,
    column_buf, turned_buf, mat_hi, mat_lo, load_sem, send_sem, recv_sem,
):
    n_slots, n_atoms = nbr_ref.shape
    n_border = border_ref.shape[1]
    groups = n_atoms // n_border
    n_vec = field_buf.shape[1] // 3
    n_rows = 2 * n_vec
    gx, gy = lax.axis_index("gx"), lax.axis_index("gy")

    def device(rank):
        dx, dy = offsets[rank] // 3 - 1, offsets[rank] % 3 - 1
        return lax.rem(gx + dx + count_x, count_x), lax.rem(gy + dy + count_y, count_y)

    barrier = pltpu.get_barrier_semaphore()
    for rank in range(8):
        pl.semaphore_signal(barrier, inc=1, device_id=device(rank), device_id_type=MESH)

    geo_buf[...] = jnp.zeros_like(geo_buf)
    moves = (
        (border_hbm, border_ref),
        (vn_hbm, field_buf.at[0]),
        (hn_hbm, field_buf.at[1]),
        (pos_hbm.at[0], geo_buf.at[0:1]),
        (pos_hbm.at[1], geo_buf.at[1:2]),
        (pos_hbm.at[2], geo_buf.at[2:3]),
        (spring_hbm, geo_buf.at[3:4]),
        (nbr_hbm, nbr_ref),
        (vp_hbm, field_buf.at[2]),
        (hp_hbm, field_buf.at[3]),
    )
    loads = [
        pltpu.make_async_copy(src, dst, load_sem.at[i]) for i, (src, dst) in enumerate(moves)
    ]
    for load in loads:
        load.start()
    for load in loads[:7]:
        load.wait()

    lane_group = lax.broadcasted_iota(jnp.int32, (n_rows, n_atoms), 1) // n_border
    chosen = jnp.concatenate([border_ref[...]] * groups, axis=1)
    chosen = jnp.broadcast_to(chosen, (n_rows, n_atoms))

    def copies(turn):
        return [
            pltpu.make_async_remote_copy(
                src_ref=out_buf.at[turn, (7 - rank) % 4],
                dst_ref=in_buf.at[turn, 7 - rank],
                send_sem=send_sem.at[turn, rank],
                recv_sem=recv_sem.at[turn, 7 - rank],
                device_id=device(rank),
                device_id_type=MESH,
            )
            for rank in range(8)
        ]

    def pack(turn, parts):
        taken = [jnp.take_along_axis(part, chosen, axis=1) for part in parts]
        for k in range(4):
            mixed = taken[0]
            for s in range(1, len(taken)):
                mixed = jnp.where(lane_group == (s + k) % 4, taken[s], mixed)
            out_buf[turn, k] = mixed

    def unpack(turn, s):
        tiles = []
        for half in range(2):
            mixed = in_buf[turn, 4 * half + (0 - s) % 4]
            for g in range(1, 4):
                mixed = jnp.where(lane_group == g, in_buf[turn, 4 * half + (g - s) % 4], mixed)
            tiles.append(pltpu.roll(mixed, (n_atoms - n_border * s) % n_atoms, 1) if s else mixed)
        return jnp.concatenate(tiles, axis=1)

    def fields(vec, heat):
        return [
            jnp.concatenate(
                [vec[a * n_vec : (a + 1) * n_vec], heat[a * n_vec : (a + 1) * n_vec]], axis=0
            )
            for a in range(3)
        ]

    geometry = geo_buf[...]
    row_of = lax.broadcasted_iota(jnp.int32, geometry.shape, 0)
    geometry = jnp.where(row_of == 3, jnp.sqrt(geometry), geometry)
    own_pos = geometry[0:3]
    root = geometry[3:4]
    state_one = fields(field_buf[0], field_buf[1])
    pack(0, state_one + [geometry])

    loads[7].wait()
    entries = nbr_ref[...]
    shift = n_atoms.bit_length() - 1
    small = n_border.bit_length() - 1
    offset = entries >> shift
    within = entries & (n_atoms - 1)
    block = jnp.where(
        offset == 4, within >> small, jnp.where(offset > 4, offset + groups - 1, offset + groups)
    )
    word = (block >> 2) * n_border + (within & (n_border - 1))
    key_buf[...] = jnp.where(entries < 0, -1, word)
    amount_buf[...] = jnp.left_shift(jnp.int32(1), (block & 3) * 8)
    n_words = 3 * n_border
    numbers = lax.broadcasted_iota(jnp.int32, (n_words, n_atoms), 0)

    def add_slots(turn, total):
        start = pl.multiple_of(turn * 8, 8)
        keys = key_buf[pl.ds(start, 8), :]
        amounts = amount_buf[pl.ds(start, 8), :]
        for n in range(8):
            total = total + jnp.where(numbers == keys[n : n + 1], amounts[n : n + 1], 0)
        return total

    words = lax.fori_loop(
        0, n_slots // 8, add_slots, jnp.zeros((n_words, n_atoms), jnp.int32)
    )
    for g in range(3):
        for f in range(4):
            row = (4 * g + f) * n_border
            part = words[g * n_border : (g + 1) * n_border]
            times_buf[row : row + n_border] = ((part >> (8 * f)) & 255).astype(jnp.float32)

    pl.semaphore_wait(barrier, 8)
    first = copies(0)
    for rank in send_order:
        first[rank].start()

    def start_of(turn):
        start = turn * n_border
        return start if isinstance(turn, int) else pl.multiple_of(start, n_border)

    def build(turn, sums, columns=None):
        group = pl.ds(start_of(turn), n_border)
        if columns is None:
            columns = column_buf[group, :]
        delta = [columns[:, a : a + 1] - own_pos[a : a + 1] for a in range(3)]
        dist_sq = delta[0] * delta[0] + delta[1] * delta[1] + delta[2] * delta[2]
        scale = times_buf[group, :] * (columns[:, 3:4] * root)
        near = dist_sq + 1.0
        share = scale / (near * (n_slots + dist_sq * (n_slots / reach_sq)))
        coupling = share * near
        bent = [(share + share) * part for part in delta]
        out = []
        for index, (a, b) in enumerate(pairs):
            entry = bent[a] * delta[b]
            if a == b:
                entry = entry + coupling
            high, low = halves(entry)
            lanes = slice(index * n_atoms, (index + 1) * n_atoms)
            mat_hi[group, lanes] = high
            mat_lo[group, lanes] = low
            out.append(sums[index] + jnp.sum(entry.reshape(-1, 8, n_atoms), axis=0))
        return tuple(out)

    def product(rows, sources):
        high, low = halves(jnp.concatenate(sources, axis=0))
        both = jnp.concatenate([high, low], axis=0)
        big = jnp.dot(both, mat_hi[rows, :], preferred_element_type=jnp.float32)
        rest = jnp.dot(high, mat_lo[rows, :], preferred_element_type=jnp.float32)
        return big[: 3 * n_rows] + big[3 * n_rows :] + rest

    def pieces(full):
        return [
            [
                full[b * n_rows : (b + 1) * n_rows, index * n_atoms : (index + 1) * n_atoms]
                for index in range(6)
            ]
            for b in range(3)
        ]

    def gathered(full):
        part = pieces(full)
        place = {pair: index for index, pair in enumerate(pairs)}
        return [
            sum(part[b][place[(min(a, b), max(a, b))]] for b in range(3)) for a in range(3)
        ]

    sums = tuple(jnp.zeros((8, n_atoms), jnp.float32) for _ in pairs)
    column_buf[...] = jnp.transpose(geometry[:8])
    sums = lax.fori_loop(0, groups, build, sums)
    home = slice(0, n_atoms)
    away = slice(n_atoms, 3 * n_atoms)
    near_part = product(home, state_one)

    lower = 2 * gy < count_y
    order = [
        rank if rank == other else jnp.where(lower, rank, other)
        for rank, other in zip((1, 6, 2, 4, 7, 0, 3, 5), (1, 6, 0, 3, 5, 2, 4, 7))
    ]
    component = lax.broadcasted_iota(jnp.int32, (1, 8), 1)

    def receive(ranks, sums):
        for rank in ranks:
            pltpu.make_async_remote_copy(
                src_ref=out_buf.at[0, 0],
                dst_ref=in_buf.at[0, rank],
                send_sem=send_sem.at[0, 0],
                recv_sem=recv_sem.at[0, rank],
                device_id=device(0),
                device_id_type=MESH,
            ).wait_recv()
        for place, rank in enumerate(ranks):
            turned_buf[place] = jnp.transpose(in_buf[0, rank, :8, :])
        for place, rank in enumerate(ranks):
            offset = rank + (rank >= 4) if isinstance(rank, int) else rank + jnp.where(rank >= 4, 1, 0)
            step_x = offset // 3 - 1
            step_y = offset - 3 * (step_x + 1) - 1
            step = jnp.where(component == 0, step_x, jnp.where(component == 1, step_y, 0))
            group = (rank + 3) % 4
            start = group * n_border
            if not isinstance(rank, int):
                start = pl.multiple_of(start, n_border)
            columns = turned_buf[place, pl.ds(start, n_border), :]
            columns = columns + step.astype(jnp.float32) * column_edge
            sums = build(groups + rank, sums, columns)
        return sums

    sums = receive(order[:5], sums)
    sums = receive(order[5:], sums)
    totals = [jnp.sum(part, axis=0, keepdims=True) for part in sums]
    weight = {pair: total for pair, total in zip(pairs, totals)}

    def stepped(state, before, far):
        out = []
        for a in range(3):
            value = sum(weight[(min(a, b), max(a, b))] * state[b] for b in range(3))
            out.append(2.0 * (value - far[a] - state[a]) - before[a])
        return out

    far = gathered(near_part + product(away, [unpack(0, s) for s in range(3)]))
    for load in loads[8:]:
        load.wait()
    state_two = stepped(state_one, fields(field_buf[2], field_buf[3]), far)
    pack(1, state_two)
    second = copies(1)
    for rank in send_order:
        second[rank].start()
    for a in range(3):
        vec_next[a * n_vec : (a + 1) * n_vec] = state_two[a][:n_vec]
        heat_next[a * n_vec : (a + 1) * n_vec] = state_two[a][n_vec:]
    near_part = product(home, state_two)
    for copy in second:
        copy.wait_recv()
    far = gathered(near_part + product(away, [unpack(1, s) for s in range(3)]))
    state_three = stepped(state_two, state_one, far)
    for a in range(3):
        vec_after[a * n_vec : (a + 1) * n_vec] = state_three[a][:n_vec]
        heat_after[a * n_vec : (a + 1) * n_vec] = state_three[a][n_vec:]
    for copy in first + second:
        copy.wait_send()


def deliver(*refs):
    sem = refs[8]
    moves = [pltpu.make_async_copy(refs[i], refs[4 + i], sem.at[i]) for i in range(4)]
    for move in moves:
        move.start()
    for move in moves:
        move.wait()


def shards(positions, spring, border, neighbours, vec_prev, vec_now, heat_prev, heat_now):
    n_atoms = spring.shape[-1]
    n_slots = neighbours.shape[2]
    n_border = border.shape[-1]
    n_vec = vec_prev.shape[1]
    n_rows = 2 * n_vec
    flat = jax.ShapeDtypeStruct((3 * n_vec, n_atoms), jnp.float32)
    vmem = pl.BlockSpec(memory_space=pltpu.VMEM)
    hbm = pl.BlockSpec(memory_space=pltpu.HBM)
    made = pl.pallas_call(
        functools.partial(kernel, lax.axis_size("gx"), lax.axis_size("gy")),
        out_shape=(pltpu.VMEM(flat.shape, flat.dtype),) * 4,
        in_specs=[hbm] * 8,
        out_specs=(vmem,) * 4,
        scratch_shapes=[
            pltpu.VMEM((n_rows, n_atoms), jnp.float32),
            pltpu.VMEM((1, n_border), jnp.int32),
            pltpu.VMEM((n_slots, n_atoms), jnp.int32),
            pltpu.VMEM((4, 3 * n_vec, n_atoms), jnp.float32),
            pltpu.VMEM((2, 4, n_rows, n_atoms), jnp.float32),
            pltpu.VMEM((2, 8, n_rows, n_atoms), jnp.float32),
            pltpu.VMEM((n_slots, n_atoms), jnp.int32),
            pltpu.VMEM((n_slots, n_atoms), jnp.int32),
            pltpu.VMEM((3 * n_atoms, n_atoms), jnp.float32),
            pltpu.VMEM((n_atoms, 8), jnp.float32),
            pltpu.VMEM((5, n_atoms, 8), jnp.float32),
            pltpu.VMEM((3 * n_atoms, 6 * n_atoms), jnp.bfloat16),
            pltpu.VMEM((3 * n_atoms, 6 * n_atoms), jnp.bfloat16),
            pltpu.SemaphoreType.DMA((10,)),
            pltpu.SemaphoreType.DMA((2, 8)),
            pltpu.SemaphoreType.DMA((2, 8)),
        ],
        compiler_params=pltpu.CompilerParams(
            collective_id=0, has_side_effects=True, vmem_limit_bytes=24 * 1024 * 1024
        ),
        name="chebyshev",
    )(
        *(
            pltpu.with_memory_space_constraint(x, pltpu.HBM)
            for x in (
                positions.reshape(3, 1, n_atoms),
                spring.reshape(1, n_atoms),
                border.reshape(1, n_border),
                neighbours.reshape(n_slots, n_atoms),
                *(x.reshape(3 * n_vec, n_atoms) for x in (vec_prev, vec_now, heat_prev, heat_now)),
            )
        ),
    )
    outs = pl.pallas_call(
        deliver,
        out_shape=(flat,) * 4,
        in_specs=[vmem] * 4,
        out_specs=(hbm,) * 4,
        scratch_shapes=[pltpu.SemaphoreType.DMA((4,))],
        name="deliver",
    )(*made)
    return tuple(out.reshape(vec_prev.shape) for out in outs)


def solution(mesh):
    fields = P(None, None, "gx", "gy", None)
    return jax.shard_map(
        shards,
        mesh=mesh,
        in_specs=(
            P(None, "gx", "gy", None),
            P("gx", "gy", None),
            P("gx", "gy", None),
            P("gx", "gy", None, None),
            fields,
            fields,
            fields,
            fields,
        ),
        out_specs=(fields,) * 4,
        check_vma=False,
    )
```

```python
import functools

import jax
import jax.numpy as jnp
from jax import lax
from jax.experimental import pallas as pl
from jax.experimental.pallas import tpu as pltpu
from jax.sharding import PartitionSpec as P

column_edge = 20.0
reach_sq = 64.0
MESH = pl.DeviceIdType.MESH
offsets = (0, 1, 2, 3, 5, 6, 7, 8)
send_order = (0, 3, 5, 2, 4, 7, 1, 6)
pairs = ((0, 0), (0, 1), (1, 1), (1, 2), (2, 2), (0, 2))


def halves(values):
    high = values.astype(jnp.bfloat16)
    return high, (values - high.astype(jnp.float32)).astype(jnp.bfloat16)


def kernel(
    count_x, count_y,
    pos_hbm, spring_hbm, border_hbm, nbr_hbm, vp_hbm, vn_hbm, hp_hbm, hn_hbm,
    vec_next, vec_after, heat_next, heat_after,
    geo_buf, border_ref, nbr_ref, field_buf, out_buf, in_buf, key_buf, amount_buf, times_buf,
    column_buf, turned_buf, mat_hi, mat_lo, load_sem, send_sem, recv_sem,
):
    n_slots, n_atoms = nbr_ref.shape
    n_border = border_ref.shape[1]
    groups = n_atoms // n_border
    n_vec = field_buf.shape[1] // 3
    n_rows = 2 * n_vec
    gx, gy = lax.axis_index("gx"), lax.axis_index("gy")

    def device(rank):
        dx, dy = offsets[rank] // 3 - 1, offsets[rank] % 3 - 1
        return lax.rem(gx + dx + count_x, count_x), lax.rem(gy + dy + count_y, count_y)

    barrier = pltpu.get_barrier_semaphore()
    for rank in send_order:
        pl.semaphore_signal(barrier, inc=1, device_id=device(rank), device_id_type=MESH)

    geo_buf[...] = jnp.zeros_like(geo_buf)
    moves = (
        (border_hbm, border_ref),
        (vn_hbm, field_buf.at[0]),
        (hn_hbm, field_buf.at[1]),
        (pos_hbm.at[0], geo_buf.at[0:1]),
        (pos_hbm.at[1], geo_buf.at[1:2]),
        (pos_hbm.at[2], geo_buf.at[2:3]),
        (spring_hbm, geo_buf.at[3:4]),
        (nbr_hbm, nbr_ref),
        (vp_hbm, field_buf.at[2]),
        (hp_hbm, field_buf.at[3]),
    )
    loads = [
        pltpu.make_async_copy(src, dst, load_sem.at[i]) for i, (src, dst) in enumerate(moves)
    ]
    for load in loads:
        load.start()
    for load in loads[:7]:
        load.wait()

    lane_group = lax.broadcasted_iota(jnp.int32, (n_rows, n_atoms), 1) // n_border
    chosen = jnp.concatenate([border_ref[...]] * groups, axis=1)
    chosen = jnp.broadcast_to(chosen, (n_rows, n_atoms))

    def copies(turn):
        return [
            pltpu.make_async_remote_copy(
                src_ref=out_buf.at[turn, (7 - rank) % 4],
                dst_ref=in_buf.at[turn, 7 - rank],
                send_sem=send_sem.at[turn, rank],
                recv_sem=recv_sem.at[turn, 7 - rank],
                device_id=device(rank),
                device_id_type=MESH,
            )
            for rank in range(8)
        ]

    def pack(turn, parts):
        taken = [jnp.take_along_axis(part, chosen, axis=1) for part in parts]
        for k in range(4):
            mixed = taken[0]
            for s in range(1, len(taken)):
                mixed = jnp.where(lane_group == (s + k) % 4, taken[s], mixed)
            out_buf[turn, k] = mixed

    def unpack(turn, s):
        tiles = []
        for half in range(2):
            mixed = in_buf[turn, 4 * half + (0 - s) % 4]
            for g in range(1, 4):
                mixed = jnp.where(lane_group == g, in_buf[turn, 4 * half + (g - s) % 4], mixed)
            tiles.append(pltpu.roll(mixed, (n_atoms - n_border * s) % n_atoms, 1) if s else mixed)
        return jnp.concatenate(tiles, axis=1)

    def fields(vec, heat):
        return [
            jnp.concatenate(
                [vec[a * n_vec : (a + 1) * n_vec], heat[a * n_vec : (a + 1) * n_vec]], axis=0
            )
            for a in range(3)
        ]

    geometry = geo_buf[...]
    row_of = lax.broadcasted_iota(jnp.int32, geometry.shape, 0)
    geometry = jnp.where(row_of == 3, jnp.sqrt(geometry), geometry)
    own_pos = geometry[0:3]
    root = geometry[3:4]
    state_one = fields(field_buf[0], field_buf[1])
    pack(0, state_one + [geometry])

    loads[7].wait()
    entries = nbr_ref[...]
    shift = n_atoms.bit_length() - 1
    small = n_border.bit_length() - 1
    offset = entries >> shift
    within = entries & (n_atoms - 1)
    block = jnp.where(
        offset == 4, within >> small, jnp.where(offset > 4, offset + groups - 1, offset + groups)
    )
    word = (block >> 2) * n_border + (within & (n_border - 1))
    key_buf[...] = jnp.where(entries < 0, -1, word)
    amount_buf[...] = jnp.left_shift(jnp.int32(1), (block & 3) * 8)
    n_words = 3 * n_border
    numbers = lax.broadcasted_iota(jnp.int32, (n_words, n_atoms), 0)

    def add_slots(turn, total):
        start = pl.multiple_of(turn * 8, 8)
        keys = key_buf[pl.ds(start, 8), :]
        amounts = amount_buf[pl.ds(start, 8), :]
        for n in range(8):
            total = total + jnp.where(numbers == keys[n : n + 1], amounts[n : n + 1], 0)
        return total

    words = lax.fori_loop(
        0, n_slots // 8, add_slots, jnp.zeros((n_words, n_atoms), jnp.int32)
    )
    for g in range(3):
        for f in range(4):
            row = (4 * g + f) * n_border
            part = words[g * n_border : (g + 1) * n_border]
            times_buf[row : row + n_border] = ((part >> (8 * f)) & 255).astype(jnp.float32)

    pl.semaphore_wait(barrier, 8)
    first = copies(0)
    for rank in send_order:
        first[rank].start()

    def start_of(turn):
        start = turn * n_border
        return start if isinstance(turn, int) else pl.multiple_of(start, n_border)

    def build(turn, sums, columns=None):
        group = pl.ds(start_of(turn), n_border)
        if columns is None:
            columns = column_buf[group, :]
        delta = [columns[:, a : a + 1] - own_pos[a : a + 1] for a in range(3)]
        dist_sq = delta[0] * delta[0] + delta[1] * delta[1] + delta[2] * delta[2]
        scale = times_buf[group, :] * (columns[:, 3:4] * root)
        near = dist_sq + 1.0
        share = scale / (near * (n_slots + dist_sq * (n_slots / reach_sq)))
        coupling = share * near
        bent = [(share + share) * part for part in delta]
        out = []
        for index, (a, b) in enumerate(pairs):
            entry = bent[a] * delta[b]
            if a == b:
                entry = entry + coupling
            high, low = halves(entry)
            lanes = slice(index * n_atoms, (index + 1) * n_atoms)
            mat_hi[group, lanes] = high
            mat_lo[group, lanes] = low
            out.append(sums[index] + jnp.sum(entry.reshape(-1, 8, n_atoms), axis=0))
        return tuple(out)

    def product(rows, sources):
        high, low = halves(jnp.concatenate(sources, axis=0))
        both = jnp.concatenate([high, low], axis=0)
        big = jnp.dot(both, mat_hi[rows, :], preferred_element_type=jnp.float32)
        rest = jnp.dot(high, mat_lo[rows, :], preferred_element_type=jnp.float32)
        return big[: 3 * n_rows] + big[3 * n_rows :] + rest

    def pieces(full):
        return [
            [
                full[b * n_rows : (b + 1) * n_rows, index * n_atoms : (index + 1) * n_atoms]
                for index in range(6)
            ]
            for b in range(3)
        ]

    def gathered(full):
        part = pieces(full)
        place = {pair: index for index, pair in enumerate(pairs)}
        return [
            sum(part[b][place[(min(a, b), max(a, b))]] for b in range(3)) for a in range(3)
        ]

    sums = tuple(jnp.zeros((8, n_atoms), jnp.float32) for _ in pairs)
    column_buf[...] = jnp.transpose(geometry[:8])
    sums = lax.fori_loop(0, groups, build, sums)
    home = slice(0, n_atoms)
    away = slice(n_atoms, 3 * n_atoms)
    near_part = product(home, state_one)

    lower = 2 * gy < count_y
    order = [
        rank if rank == other else jnp.where(lower, rank, other)
        for rank, other in zip((1, 6, 2, 4, 7, 0, 3, 5), (1, 6, 0, 3, 5, 2, 4, 7))
    ]
    component = lax.broadcasted_iota(jnp.int32, (1, 8), 1)

    def receive(ranks, sums):
        for rank in ranks:
            pltpu.make_async_remote_copy(
                src_ref=out_buf.at[0, 0],
                dst_ref=in_buf.at[0, rank],
                send_sem=send_sem.at[0, 0],
                recv_sem=recv_sem.at[0, rank],
                device_id=device(0),
                device_id_type=MESH,
            ).wait_recv()
        for place, rank in enumerate(ranks):
            turned_buf[place] = jnp.transpose(in_buf[0, rank, :8, :])
        for place, rank in enumerate(ranks):
            offset = rank + (rank >= 4) if isinstance(rank, int) else rank + jnp.where(rank >= 4, 1, 0)
            step_x = offset // 3 - 1
            step_y = offset - 3 * (step_x + 1) - 1
            step = jnp.where(component == 0, step_x, jnp.where(component == 1, step_y, 0))
            group = (rank + 3) % 4
            start = group * n_border
            if not isinstance(rank, int):
                start = pl.multiple_of(start, n_border)
            columns = turned_buf[place, pl.ds(start, n_border), :]
            columns = columns + step.astype(jnp.float32) * column_edge
            sums = build(groups + rank, sums, columns)
        return sums

    sums = receive(order[:5], sums)
    sums = receive(order[5:], sums)
    totals = [jnp.sum(part, axis=0, keepdims=True) for part in sums]
    weight = {pair: total for pair, total in zip(pairs, totals)}

    def stepped(state, before, far):
        out = []
        for a in range(3):
            value = sum(weight[(min(a, b), max(a, b))] * state[b] for b in range(3))
            out.append(2.0 * (value - far[a] - state[a]) - before[a])
        return out

    far = gathered(near_part + product(away, [unpack(0, s) for s in range(3)]))
    for load in loads[8:]:
        load.wait()
    state_two = stepped(state_one, fields(field_buf[2], field_buf[3]), far)
    pack(1, state_two)
    second = copies(1)
    for rank in send_order:
        second[rank].start()
    for a in range(3):
        vec_next[a * n_vec : (a + 1) * n_vec] = state_two[a][:n_vec]
        heat_next[a * n_vec : (a + 1) * n_vec] = state_two[a][n_vec:]
    near_part = product(home, state_two)
    for copy in second:
        copy.wait_recv()
    far = gathered(near_part + product(away, [unpack(1, s) for s in range(3)]))
    state_three = stepped(state_two, state_one, far)
    for a in range(3):
        vec_after[a * n_vec : (a + 1) * n_vec] = state_three[a][:n_vec]
        heat_after[a * n_vec : (a + 1) * n_vec] = state_three[a][n_vec:]
    for copy in first + second:
        copy.wait_send()


def deliver(*refs):
    sem = refs[8]
    moves = [pltpu.make_async_copy(refs[i], refs[4 + i], sem.at[i]) for i in range(4)]
    for move in moves:
        move.start()
    for move in moves:
        move.wait()


def shards(positions, spring, border, neighbours, vec_prev, vec_now, heat_prev, heat_now):
    n_atoms = spring.shape[-1]
    n_slots = neighbours.shape[2]
    n_border = border.shape[-1]
    n_vec = vec_prev.shape[1]
    n_rows = 2 * n_vec
    flat = jax.ShapeDtypeStruct((3 * n_vec, n_atoms), jnp.float32)
    vmem = pl.BlockSpec(memory_space=pltpu.VMEM)
    hbm = pl.BlockSpec(memory_space=pltpu.HBM)
    made = pl.pallas_call(
        functools.partial(kernel, lax.axis_size("gx"), lax.axis_size("gy")),
        out_shape=(pltpu.VMEM(flat.shape, flat.dtype),) * 4,
        in_specs=[hbm] * 8,
        out_specs=(vmem,) * 4,
        scratch_shapes=[
            pltpu.VMEM((n_rows, n_atoms), jnp.float32),
            pltpu.VMEM((1, n_border), jnp.int32),
            pltpu.VMEM((n_slots, n_atoms), jnp.int32),
            pltpu.VMEM((4, 3 * n_vec, n_atoms), jnp.float32),
            pltpu.VMEM((2, 4, n_rows, n_atoms), jnp.float32),
            pltpu.VMEM((2, 8, n_rows, n_atoms), jnp.float32),
            pltpu.VMEM((n_slots, n_atoms), jnp.int32),
            pltpu.VMEM((n_slots, n_atoms), jnp.int32),
            pltpu.VMEM((3 * n_atoms, n_atoms), jnp.float32),
            pltpu.VMEM((n_atoms, 8), jnp.float32),
            pltpu.VMEM((5, n_atoms, 8), jnp.float32),
            pltpu.VMEM((3 * n_atoms, 6 * n_atoms), jnp.bfloat16),
            pltpu.VMEM((3 * n_atoms, 6 * n_atoms), jnp.bfloat16),
            pltpu.SemaphoreType.DMA((10,)),
            pltpu.SemaphoreType.DMA((2, 8)),
            pltpu.SemaphoreType.DMA((2, 8)),
        ],
        compiler_params=pltpu.CompilerParams(
            collective_id=0, has_side_effects=True, vmem_limit_bytes=24 * 1024 * 1024
        ),
        name="chebyshev",
    )(
        *(
            pltpu.with_memory_space_constraint(x, pltpu.HBM)
            for x in (
                positions.reshape(3, 1, n_atoms),
                spring.reshape(1, n_atoms),
                border.reshape(1, n_border),
                neighbours.reshape(n_slots, n_atoms),
                *(x.reshape(3 * n_vec, n_atoms) for x in (vec_prev, vec_now, heat_prev, heat_now)),
            )
        ),
    )
    outs = pl.pallas_call(
        deliver,
        out_shape=(flat,) * 4,
        in_specs=[vmem] * 4,
        out_specs=(hbm,) * 4,
        scratch_shapes=[pltpu.SemaphoreType.DMA((4,))],
        name="deliver",
    )(*(pltpu.with_memory_space_constraint(x, pltpu.VMEM) for x in made))
    return tuple(out.reshape(vec_prev.shape) for out in outs)


def solution(mesh):
    fields = P(None, None, "gx", "gy", None)
    return jax.shard_map(
        shards,
        mesh=mesh,
        in_specs=(
            P(None, "gx", "gy", None),
            P("gx", "gy", None),
            P("gx", "gy", None),
            P("gx", "gy", None, None),
            fields,
            fields,
            fields,
            fields,
        ),
        out_specs=(fields,) * 4,
        check_vma=False,
    )
```

```python
import functools

import jax
import jax.numpy as jnp
from jax import lax
from jax.experimental import pallas as pl
from jax.experimental.pallas import tpu as pltpu
from jax.sharding import PartitionSpec as P

column_edge = 20.0
reach_sq = 64.0
MESH = pl.DeviceIdType.MESH
offsets = (0, 1, 2, 3, 5, 6, 7, 8)
send_order = (0, 3, 5, 2, 4, 7, 1, 6)
arrivals = ((1, 6, 2, 4, 7, 0, 3, 5), (1, 6, 0, 3, 5, 2, 4, 7))
pairs = ((0, 0), (0, 1), (1, 1), (1, 2), (2, 2), (0, 2))


def halves(values):
    high = values.astype(jnp.bfloat16)
    return high, (values - high.astype(jnp.float32)).astype(jnp.bfloat16)


def kernel(
    count_x, count_y,
    pos_hbm, spring_hbm, border_hbm, nbr_hbm, vp_hbm, vn_hbm, hp_hbm, hn_hbm,
    vec_next, vec_after, heat_next, heat_after,
    geo_buf, border_ref, nbr_ref, field_buf, out_buf, in_buf, key_buf, amount_buf, times_buf,
    column_buf, mat_hi, mat_lo, load_sem, send_sem, recv_sem,
):
    n_slots, n_atoms = nbr_ref.shape
    n_border = border_ref.shape[1]
    groups = n_atoms // n_border
    n_vec = field_buf.shape[1] // 3
    n_rows = 2 * n_vec
    gx, gy = lax.axis_index("gx"), lax.axis_index("gy")

    def device(rank):
        dx, dy = offsets[rank] // 3 - 1, offsets[rank] % 3 - 1
        return lax.rem(gx + dx + count_x, count_x), lax.rem(gy + dy + count_y, count_y)

    barrier = pltpu.get_barrier_semaphore()
    for rank in send_order:
        pl.semaphore_signal(barrier, inc=1, device_id=device(rank), device_id_type=MESH)

    geo_buf[...] = jnp.zeros_like(geo_buf)
    moves = (
        (border_hbm, border_ref),
        (vn_hbm, field_buf.at[0]),
        (hn_hbm, field_buf.at[1]),
        (pos_hbm.at[0], geo_buf.at[0:1]),
        (pos_hbm.at[1], geo_buf.at[1:2]),
        (pos_hbm.at[2], geo_buf.at[2:3]),
        (spring_hbm, geo_buf.at[3:4]),
        (nbr_hbm, nbr_ref),
        (vp_hbm, field_buf.at[2]),
        (hp_hbm, field_buf.at[3]),
    )
    loads = [
        pltpu.make_async_copy(src, dst, load_sem.at[i]) for i, (src, dst) in enumerate(moves)
    ]
    for load in loads:
        load.start()
    for load in loads[:7]:
        load.wait()

    lane_group = lax.broadcasted_iota(jnp.int32, (n_rows, n_atoms), 1) // n_border
    chosen = jnp.concatenate([border_ref[...]] * groups, axis=1)
    chosen = jnp.broadcast_to(chosen, (n_rows, n_atoms))

    def copies(turn):
        return [
            pltpu.make_async_remote_copy(
                src_ref=out_buf.at[turn, place % 4],
                dst_ref=in_buf.at[turn, place],
                send_sem=send_sem.at[turn, rank],
                recv_sem=recv_sem.at[turn, place],
                device_id=device(rank),
                device_id_type=MESH,
            )
            for rank, place in enumerate(places)
        ]

    def either(low, one, other):
        return one if one == other else jnp.where(low, one, other)

    places = [
        either(2 * device(rank)[1] < count_y, *(order.index(7 - rank) for order in arrivals))
        for rank in range(8)
    ]

    def arrive(turn, first, last):
        for place in range(first, last):
            pltpu.make_async_remote_copy(
                src_ref=out_buf.at[turn, 0],
                dst_ref=in_buf.at[turn, place],
                send_sem=send_sem.at[turn, 0],
                recv_sem=recv_sem.at[turn, place],
                device_id=device(0),
                device_id_type=MESH,
            ).wait_recv()

    def pack(turn, parts):
        taken = [jnp.take_along_axis(part, chosen, axis=1) for part in parts]
        for k in range(4):
            mixed = taken[0]
            for s in range(1, len(taken)):
                mixed = jnp.where(lane_group == (s + k) % 4, taken[s], mixed)
            out_buf[turn, k] = mixed

    def unpack(turn, half):
        tiles = []
        for s in range(3):
            mixed = in_buf[turn, 4 * half + (0 - s) % 4]
            for g in range(1, 4):
                mixed = jnp.where(lane_group == g, in_buf[turn, 4 * half + (g - s) % 4], mixed)
            tiles.append(pltpu.roll(mixed, (n_atoms - n_border * s) % n_atoms, 1) if s else mixed)
        return tiles

    def fields(vec, heat):
        return [
            jnp.concatenate(
                [vec[a * n_vec : (a + 1) * n_vec], heat[a * n_vec : (a + 1) * n_vec]], axis=0
            )
            for a in range(3)
        ]

    geometry = geo_buf[...]
    row_of = lax.broadcasted_iota(jnp.int32, geometry.shape, 0)
    geometry = jnp.where(row_of == 3, jnp.sqrt(geometry), geometry)
    own_pos = geometry[0:3]
    root = geometry[3:4]
    state_one = fields(field_buf[0], field_buf[1])
    pack(0, state_one + [geometry])

    loads[7].wait()
    entries = nbr_ref[...]
    shift = n_atoms.bit_length() - 1
    small = n_border.bit_length() - 1
    offset = entries >> shift
    within = entries & (n_atoms - 1)
    block = jnp.where(
        offset == 4, within >> small, jnp.where(offset > 4, offset + groups - 1, offset + groups)
    )
    word = (block >> 2) * n_border + (within & (n_border - 1))
    key_buf[...] = jnp.where(entries < 0, -1, word)
    amount_buf[...] = jnp.left_shift(jnp.int32(1), (block & 3) * 8)
    n_words = 3 * n_border
    numbers = lax.broadcasted_iota(jnp.int32, (n_words, n_atoms), 0)

    def add_slots(turn, total):
        start = pl.multiple_of(turn * 8, 8)
        keys = key_buf[pl.ds(start, 8), :]
        amounts = amount_buf[pl.ds(start, 8), :]
        for n in range(8):
            total = total + jnp.where(numbers == keys[n : n + 1], amounts[n : n + 1], 0)
        return total

    words = lax.fori_loop(
        0, n_slots // 8, add_slots, jnp.zeros((n_words, n_atoms), jnp.int32)
    )
    for g in range(3):
        for f in range(4):
            row = (4 * g + f) * n_border
            part = words[g * n_border : (g + 1) * n_border]
            times_buf[row : row + n_border] = ((part >> (8 * f)) & 255).astype(jnp.float32)

    pl.semaphore_wait(barrier, 8)
    first = copies(0)
    for rank in send_order:
        first[rank].start()

    def slots_of(turn):
        start = turn * n_border
        return pl.ds(start if isinstance(turn, int) else pl.multiple_of(start, n_border), n_border)

    def build(group, counts, columns, sums):
        delta = [columns[:, a : a + 1] - own_pos[a : a + 1] for a in range(3)]
        dist_sq = delta[0] * delta[0] + delta[1] * delta[1] + delta[2] * delta[2]
        scale = times_buf[counts, :] * (columns[:, 3:4] * root)
        near = dist_sq + 1.0
        share = scale / (near * (n_slots + dist_sq * (n_slots / reach_sq)))
        coupling = share * near
        bent = [(share + share) * part for part in delta]
        out = []
        for index, (a, b) in enumerate(pairs):
            entry = bent[a] * delta[b]
            if a == b:
                entry = entry + coupling
            high, low = halves(entry)
            lanes = slice(index * n_atoms, (index + 1) * n_atoms)
            mat_hi[group, lanes] = high
            mat_lo[group, lanes] = low
            out.append(sums[index] + jnp.sum(entry.reshape(-1, 8, n_atoms), axis=0))
        return tuple(out)

    def product(tile, sources):
        rows = slice(tile * n_atoms, (tile + 1) * n_atoms)
        high, low = halves(jnp.concatenate(sources, axis=0))
        both = jnp.concatenate([high, low], axis=0)
        big = jnp.dot(both, mat_hi[rows, :], preferred_element_type=jnp.float32)
        rest = jnp.dot(high, mat_lo[rows, :], preferred_element_type=jnp.float32)
        return big[: 3 * n_rows] + big[3 * n_rows :] + rest

    def pieces(full):
        return [
            [
                full[b * n_rows : (b + 1) * n_rows, index * n_atoms : (index + 1) * n_atoms]
                for index in range(6)
            ]
            for b in range(3)
        ]

    def gathered(full):
        part = pieces(full)
        place = {pair: index for index, pair in enumerate(pairs)}
        return [
            sum(part[b][place[(min(a, b), max(a, b))]] for b in range(3)) for a in range(3)
        ]

    sums = tuple(jnp.zeros((8, n_atoms), jnp.float32) for _ in pairs)
    column_buf[...] = jnp.transpose(geometry[:8])

    def build_own(turn, sums):
        group = slots_of(turn)
        return build(group, group, column_buf[group, :], sums)

    sums = lax.fori_loop(0, groups, build_own, sums)
    total = product(0, state_one)

    lower = 2 * gy < count_y
    component = lax.broadcasted_iota(jnp.int32, (1, 8), 1)

    def receive(first, last, sums):
        arrive(0, first, last)
        turned = [jnp.transpose(in_buf[0, place, :8, :]) for place in range(first, last)]
        for place in range(first, last):
            rank = either(lower, *(order[place] for order in arrivals))
            offset = rank + jnp.where(jnp.int32(rank) >= 4, 1, 0)
            step_x = offset // 3 - 1
            step_y = offset - 3 * (step_x + 1) - 1
            step = jnp.where(component == 0, step_x, jnp.where(component == 1, step_y, 0))
            start = (place + 3) % 4 * n_border
            columns = turned[place - first][start : start + n_border]
            columns = columns + step.astype(jnp.float32) * column_edge
            sums = build(slots_of(groups + place), slots_of(groups + rank), columns, sums)
        return sums

    sums = receive(0, 5, sums)
    total = total + product(1, unpack(0, 0))
    sums = receive(5, 8, sums)
    totals = [jnp.sum(part, axis=0, keepdims=True) for part in sums]
    weight = {pair: total for pair, total in zip(pairs, totals)}

    def stepped(state, before, far):
        out = []
        for a in range(3):
            value = sum(weight[(min(a, b), max(a, b))] * state[b] for b in range(3))
            out.append(2.0 * (value - far[a] - state[a]) - before[a])
        return out

    far = gathered(total + product(2, unpack(0, 1)))
    for load in loads[8:]:
        load.wait()
    state_two = stepped(state_one, fields(field_buf[2], field_buf[3]), far)
    pack(1, state_two)
    second = copies(1)
    for rank in send_order:
        second[rank].start()
    for a in range(3):
        vec_next[a * n_vec : (a + 1) * n_vec] = state_two[a][:n_vec]
        heat_next[a * n_vec : (a + 1) * n_vec] = state_two[a][n_vec:]
    total = product(0, state_two)
    arrive(1, 0, 4)
    total = total + product(1, unpack(1, 0))
    arrive(1, 4, 8)
    far = gathered(total + product(2, unpack(1, 1)))
    state_three = stepped(state_two, state_one, far)
    for a in range(3):
        vec_after[a * n_vec : (a + 1) * n_vec] = state_three[a][:n_vec]
        heat_after[a * n_vec : (a + 1) * n_vec] = state_three[a][n_vec:]
    for copy in first + second:
        copy.wait_send()


def deliver(*refs):
    sem = refs[8]
    moves = [pltpu.make_async_copy(refs[i], refs[4 + i], sem.at[i]) for i in range(4)]
    for move in moves:
        move.start()
    for move in moves:
        move.wait()


def shards(positions, spring, border, neighbours, vec_prev, vec_now, heat_prev, heat_now):
    n_atoms = spring.shape[-1]
    n_slots = neighbours.shape[2]
    n_border = border.shape[-1]
    n_vec = vec_prev.shape[1]
    n_rows = 2 * n_vec
    flat = jax.ShapeDtypeStruct((3 * n_vec, n_atoms), jnp.float32)
    vmem = pl.BlockSpec(memory_space=pltpu.VMEM)
    hbm = pl.BlockSpec(memory_space=pltpu.HBM)
    made = pl.pallas_call(
        functools.partial(kernel, lax.axis_size("gx"), lax.axis_size("gy")),
        out_shape=(pltpu.VMEM(flat.shape, flat.dtype),) * 4,
        in_specs=[hbm] * 8,
        out_specs=(vmem,) * 4,
        scratch_shapes=[
            pltpu.VMEM((n_rows, n_atoms), jnp.float32),
            pltpu.VMEM((1, n_border), jnp.int32),
            pltpu.VMEM((n_slots, n_atoms), jnp.int32),
            pltpu.VMEM((4, 3 * n_vec, n_atoms), jnp.float32),
            pltpu.VMEM((2, 4, n_rows, n_atoms), jnp.float32),
            pltpu.VMEM((2, 8, n_rows, n_atoms), jnp.float32),
            pltpu.VMEM((n_slots, n_atoms), jnp.int32),
            pltpu.VMEM((n_slots, n_atoms), jnp.int32),
            pltpu.VMEM((3 * n_atoms, n_atoms), jnp.float32),
            pltpu.VMEM((n_atoms, 8), jnp.float32),
            pltpu.VMEM((3 * n_atoms, 6 * n_atoms), jnp.bfloat16),
            pltpu.VMEM((3 * n_atoms, 6 * n_atoms), jnp.bfloat16),
            pltpu.SemaphoreType.DMA((10,)),
            pltpu.SemaphoreType.DMA((2, 8)),
            pltpu.SemaphoreType.DMA((2, 8)),
        ],
        compiler_params=pltpu.CompilerParams(
            collective_id=0, has_side_effects=True, vmem_limit_bytes=24 * 1024 * 1024
        ),
        name="chebyshev",
    )(
        *(
            pltpu.with_memory_space_constraint(x, pltpu.HBM)
            for x in (
                positions.reshape(3, 1, n_atoms),
                spring.reshape(1, n_atoms),
                border.reshape(1, n_border),
                neighbours.reshape(n_slots, n_atoms),
                *(x.reshape(3 * n_vec, n_atoms) for x in (vec_prev, vec_now, heat_prev, heat_now)),
            )
        ),
    )
    outs = pl.pallas_call(
        deliver,
        out_shape=(flat,) * 4,
        in_specs=[vmem] * 4,
        out_specs=(hbm,) * 4,
        scratch_shapes=[pltpu.SemaphoreType.DMA((4,))],
        name="deliver",
    )(*(pltpu.with_memory_space_constraint(x, pltpu.VMEM) for x in made))
    return tuple(out.reshape(vec_prev.shape) for out in outs)


def solution(mesh):
    fields = P(None, None, "gx", "gy", None)
    return jax.shard_map(
        shards,
        mesh=mesh,
        in_specs=(
            P(None, "gx", "gy", None),
            P("gx", "gy", None),
            P("gx", "gy", None),
            P("gx", "gy", None, None),
            fields,
            fields,
            fields,
            fields,
        ),
        out_specs=(fields,) * 4,
        check_vma=False,
    )
```

```python
import functools

import jax
import jax.numpy as jnp
from jax import lax
from jax.experimental import pallas as pl
from jax.experimental.pallas import tpu as pltpu
from jax.sharding import PartitionSpec as P

column_edge = 20.0
reach_sq = 64.0
MESH = pl.DeviceIdType.MESH
offsets = (0, 1, 2, 3, 5, 6, 7, 8)
departures = (5, 6, 7, 2, 3, 4, 0, 1)
arrivals = ((1, 6, 2, 4, 7, 0, 3, 5), (1, 6, 0, 3, 5, 2, 4, 7))
pairs = ((0, 0), (0, 1), (1, 1), (1, 2), (2, 2), (0, 2))


def halves(values):
    high = values.astype(jnp.bfloat16)
    return high, (values - high.astype(jnp.float32)).astype(jnp.bfloat16)


def kernel(
    count_x, count_y,
    pos_hbm, spring_hbm, border_hbm, nbr_hbm, vp_hbm, vn_hbm, hp_hbm, hn_hbm,
    vec_next, vec_after, heat_next, heat_after,
    geo_buf, border_ref, nbr_ref, field_buf, out_buf, in_buf, key_buf, amount_buf, times_buf,
    mat_hi, mat_lo, load_sem, send_sem, recv_sem,
):
    n_slots, n_atoms = nbr_ref.shape
    n_border = border_ref.shape[1]
    groups = n_atoms // n_border
    n_vec = field_buf.shape[1] // 3
    n_rows = 2 * n_vec
    gx, gy = lax.axis_index("gx"), lax.axis_index("gy")

    def device(rank):
        dx, dy = offsets[rank] // 3 - 1, offsets[rank] % 3 - 1
        return lax.rem(gx + dx + count_x, count_x), lax.rem(gy + dy + count_y, count_y)

    def either(low, one, other):
        return one if isinstance(one, int) and one == other else jnp.where(low, one, other)

    lower = 2 * gy < count_y
    places = [
        either(2 * device(rank)[1] < count_y, *(order.index(7 - rank) for order in arrivals))
        for rank in range(8)
    ]
    targets = []
    for turn in departures:
        one, other = (order[turn] for order in arrivals)
        if one == other:
            targets.append((device(one), places[one]))
        else:
            targets.append((
                tuple(jnp.where(lower, x, y) for x, y in zip(device(one), device(other))),
                jnp.where(lower, places[one], places[other]),
            ))

    barrier = pltpu.get_barrier_semaphore()
    for target, _ in targets:
        pl.semaphore_signal(barrier, inc=1, device_id=target, device_id_type=MESH)

    geo_buf[...] = jnp.zeros_like(geo_buf)
    moves = (
        (border_hbm, border_ref),
        (vn_hbm, field_buf.at[0]),
        (hn_hbm, field_buf.at[1]),
        (pos_hbm.at[0], geo_buf.at[0:1]),
        (pos_hbm.at[1], geo_buf.at[1:2]),
        (pos_hbm.at[2], geo_buf.at[2:3]),
        (spring_hbm, geo_buf.at[3:4]),
        (nbr_hbm, nbr_ref),
        (vp_hbm, field_buf.at[2]),
        (hp_hbm, field_buf.at[3]),
    )
    loads = [
        pltpu.make_async_copy(src, dst, load_sem.at[i]) for i, (src, dst) in enumerate(moves)
    ]
    for load in loads:
        load.start()
    for load in loads[:7]:
        load.wait()

    lane_group = lax.broadcasted_iota(jnp.int32, (n_rows, n_atoms), 1) // n_border
    chosen = jnp.concatenate([border_ref[...]] * groups, axis=1)
    chosen = jnp.broadcast_to(chosen, (n_rows, n_atoms))

    def copies(turn):
        return [
            pltpu.make_async_remote_copy(
                src_ref=out_buf.at[turn, place % 4],
                dst_ref=in_buf.at[turn, place],
                send_sem=send_sem.at[turn, index],
                recv_sem=recv_sem.at[turn, place],
                device_id=target,
                device_id_type=MESH,
            )
            for index, (target, place) in enumerate(targets)
        ]

    def arrive(turn, first, last):
        for place in range(first, last):
            pltpu.make_async_remote_copy(
                src_ref=out_buf.at[turn, 0],
                dst_ref=in_buf.at[turn, place],
                send_sem=send_sem.at[turn, 0],
                recv_sem=recv_sem.at[turn, place],
                device_id=device(0),
                device_id_type=MESH,
            ).wait_recv()

    def pack(turn, parts):
        taken = [jnp.take_along_axis(part, chosen, axis=1) for part in parts]
        for k in range(4):
            mixed = taken[0]
            for s in range(1, len(taken)):
                mixed = jnp.where(lane_group == (s + k) % 4, taken[s], mixed)
            out_buf[turn, k] = mixed

    def unpack(turn, half):
        tiles = []
        for s in range(3):
            mixed = in_buf[turn, 4 * half + (0 - s) % 4]
            for g in range(1, 4):
                mixed = jnp.where(lane_group == g, in_buf[turn, 4 * half + (g - s) % 4], mixed)
            tiles.append(pltpu.roll(mixed, (n_atoms - n_border * s) % n_atoms, 1) if s else mixed)
        return tiles

    def fields(vec, heat):
        return [
            jnp.concatenate(
                [vec[a * n_vec : (a + 1) * n_vec], heat[a * n_vec : (a + 1) * n_vec]], axis=0
            )
            for a in range(3)
        ]

    geometry = geo_buf[...]
    row_of = lax.broadcasted_iota(jnp.int32, geometry.shape, 0)
    geometry = jnp.where(row_of == 3, jnp.sqrt(geometry), geometry)
    own_pos = geometry[0:3]
    root = geometry[3:4]
    state_one = fields(field_buf[0], field_buf[1])
    pack(0, state_one + [geometry])

    loads[7].wait()
    entries = nbr_ref[...]
    shift = n_atoms.bit_length() - 1
    small = n_border.bit_length() - 1
    offset = entries >> shift
    within = entries & (n_atoms - 1)
    block = jnp.where(
        offset == 4, within >> small, jnp.where(offset > 4, offset + groups - 1, offset + groups)
    )
    word = (block >> 2) * n_border + (within & (n_border - 1))
    key_buf[...] = jnp.where(entries < 0, -1, word)
    amount_buf[...] = jnp.left_shift(jnp.int32(1), (block & 3) * 8)
    n_words = 3 * n_border
    numbers = lax.broadcasted_iota(jnp.int32, (n_words, n_atoms), 0)

    def add_slots(turn, total):
        start = pl.multiple_of(turn * 8, 8)
        keys = key_buf[pl.ds(start, 8), :]
        amounts = amount_buf[pl.ds(start, 8), :]
        for n in range(8):
            total = total + jnp.where(numbers == keys[n : n + 1], amounts[n : n + 1], 0)
        return total

    words = lax.fori_loop(
        0, n_slots // 8, add_slots, jnp.zeros((n_words, n_atoms), jnp.int32)
    )
    for g in range(3):
        for f in range(4):
            row = (4 * g + f) * n_border
            part = words[g * n_border : (g + 1) * n_border]
            times_buf[row : row + n_border] = ((part >> (8 * f)) & 255).astype(jnp.float32)

    pl.semaphore_wait(barrier, 8)
    first = copies(0)
    for copy in first:
        copy.start()

    def slots_of(turn):
        start = turn * n_border
        return pl.ds(start if isinstance(turn, int) else pl.multiple_of(start, n_border), n_border)

    def build(group, counts, columns, sums):
        delta = [columns[:, a : a + 1] - own_pos[a : a + 1] for a in range(3)]
        dist_sq = delta[0] * delta[0] + delta[1] * delta[1] + delta[2] * delta[2]
        scale = times_buf[counts, :] * (columns[:, 3:4] * root)
        near = dist_sq + 1.0
        share = scale / (near * (n_slots + dist_sq * (n_slots / reach_sq)))
        coupling = share * near
        bent = [(share + share) * part for part in delta]
        out = []
        for index, (a, b) in enumerate(pairs):
            entry = bent[a] * delta[b]
            if a == b:
                entry = entry + coupling
            high, low = halves(entry)
            lanes = slice(index * n_atoms, (index + 1) * n_atoms)
            mat_hi[group, lanes] = high
            mat_lo[group, lanes] = low
            out.append(sums[index] + jnp.sum(entry.reshape(-1, 8, n_atoms), axis=0))
        return tuple(out)

    def product(tile, sources):
        rows = slice(tile * n_atoms, (tile + 1) * n_atoms)
        high, low = halves(jnp.concatenate(sources, axis=0))
        both = jnp.concatenate([high, low], axis=0)
        big = jnp.dot(both, mat_hi[rows, :], preferred_element_type=jnp.float32)
        rest = jnp.dot(high, mat_lo[rows, :], preferred_element_type=jnp.float32)
        return big[: 3 * n_rows] + big[3 * n_rows :] + rest

    def pieces(full):
        return [
            [
                full[b * n_rows : (b + 1) * n_rows, index * n_atoms : (index + 1) * n_atoms]
                for index in range(6)
            ]
            for b in range(3)
        ]

    def gathered(full):
        part = pieces(full)
        place = {pair: index for index, pair in enumerate(pairs)}
        return [
            sum(part[b][place[(min(a, b), max(a, b))]] for b in range(3)) for a in range(3)
        ]

    sums = tuple(jnp.zeros((8, n_atoms), jnp.float32) for _ in pairs)
    columns = jnp.transpose(geometry[:8])
    for turn in range(groups):
        group = slots_of(turn)
        sums = build(group, group, columns[turn * n_border : (turn + 1) * n_border], sums)
    total = product(0, state_one)

    component = lax.broadcasted_iota(jnp.int32, (1, 8), 1)

    def receive(first, last, sums):
        arrive(0, first, last)
        turned = [jnp.transpose(in_buf[0, place, :8, :]) for place in range(first, last)]
        for place in range(first, last):
            rank = either(lower, *(order[place] for order in arrivals))
            offset = rank + jnp.where(jnp.int32(rank) >= 4, 1, 0)
            step_x = offset // 3 - 1
            step_y = offset - 3 * (step_x + 1) - 1
            step = jnp.where(component == 0, step_x, jnp.where(component == 1, step_y, 0))
            start = (place + 3) % 4 * n_border
            columns = turned[place - first][start : start + n_border]
            columns = columns + step.astype(jnp.float32) * column_edge
            sums = build(slots_of(groups + place), slots_of(groups + rank), columns, sums)
        return sums

    sums = receive(0, 5, sums)
    total = total + product(1, unpack(0, 0))
    sums = receive(5, 8, sums)
    totals = [jnp.sum(part, axis=0, keepdims=True) for part in sums]
    weight = {pair: total for pair, total in zip(pairs, totals)}

    def stepped(state, before, far):
        out = []
        for a in range(3):
            value = sum(weight[(min(a, b), max(a, b))] * state[b] for b in range(3))
            out.append(2.0 * (value - far[a] - state[a]) - before[a])
        return out

    far = gathered(total + product(2, unpack(0, 1)))
    for load in loads[8:]:
        load.wait()
    state_two = stepped(state_one, fields(field_buf[2], field_buf[3]), far)
    pack(1, state_two)
    second = copies(1)
    for copy in second:
        copy.start()
    for a in range(3):
        vec_next[a * n_vec : (a + 1) * n_vec] = state_two[a][:n_vec]
        heat_next[a * n_vec : (a + 1) * n_vec] = state_two[a][n_vec:]
    total = product(0, state_two)
    arrive(1, 0, 4)
    total = total + product(1, unpack(1, 0))
    arrive(1, 4, 8)
    far = gathered(total + product(2, unpack(1, 1)))
    state_three = stepped(state_two, state_one, far)
    for a in range(3):
        vec_after[a * n_vec : (a + 1) * n_vec] = state_three[a][:n_vec]
        heat_after[a * n_vec : (a + 1) * n_vec] = state_three[a][n_vec:]
    for copy in first + second:
        copy.wait_send()


def deliver(*refs):
    sem = refs[8]
    moves = [pltpu.make_async_copy(refs[i], refs[4 + i], sem.at[i]) for i in range(4)]
    for move in moves:
        move.start()
    for move in moves:
        move.wait()


def shards(positions, spring, border, neighbours, vec_prev, vec_now, heat_prev, heat_now):
    n_atoms = spring.shape[-1]
    n_slots = neighbours.shape[2]
    n_border = border.shape[-1]
    n_vec = vec_prev.shape[1]
    n_rows = 2 * n_vec
    flat = jax.ShapeDtypeStruct((3 * n_vec, n_atoms), jnp.float32)
    vmem = pl.BlockSpec(memory_space=pltpu.VMEM)
    hbm = pl.BlockSpec(memory_space=pltpu.HBM)
    made = pl.pallas_call(
        functools.partial(kernel, lax.axis_size("gx"), lax.axis_size("gy")),
        out_shape=(pltpu.VMEM(flat.shape, flat.dtype),) * 4,
        in_specs=[hbm] * 8,
        out_specs=(vmem,) * 4,
        scratch_shapes=[
            pltpu.VMEM((n_rows, n_atoms), jnp.float32),
            pltpu.VMEM((1, n_border), jnp.int32),
            pltpu.VMEM((n_slots, n_atoms), jnp.int32),
            pltpu.VMEM((4, 3 * n_vec, n_atoms), jnp.float32),
            pltpu.VMEM((2, 4, n_rows, n_atoms), jnp.float32),
            pltpu.VMEM((2, 8, n_rows, n_atoms), jnp.float32),
            pltpu.VMEM((n_slots, n_atoms), jnp.int32),
            pltpu.VMEM((n_slots, n_atoms), jnp.int32),
            pltpu.VMEM((3 * n_atoms, n_atoms), jnp.float32),
            pltpu.VMEM((3 * n_atoms, 6 * n_atoms), jnp.bfloat16),
            pltpu.VMEM((3 * n_atoms, 6 * n_atoms), jnp.bfloat16),
            pltpu.SemaphoreType.DMA((10,)),
            pltpu.SemaphoreType.DMA((2, 8)),
            pltpu.SemaphoreType.DMA((2, 8)),
        ],
        compiler_params=pltpu.CompilerParams(
            collective_id=0, has_side_effects=True, vmem_limit_bytes=24 * 1024 * 1024
        ),
        name="chebyshev",
    )(
        *(
            pltpu.with_memory_space_constraint(x, pltpu.HBM)
            for x in (
                positions.reshape(3, 1, n_atoms),
                spring.reshape(1, n_atoms),
                border.reshape(1, n_border),
                neighbours.reshape(n_slots, n_atoms),
                *(x.reshape(3 * n_vec, n_atoms) for x in (vec_prev, vec_now, heat_prev, heat_now)),
            )
        ),
    )
    outs = pl.pallas_call(
        deliver,
        out_shape=(flat,) * 4,
        in_specs=[vmem] * 4,
        out_specs=(hbm,) * 4,
        scratch_shapes=[pltpu.SemaphoreType.DMA((4,))],
        name="deliver",
    )(*(pltpu.with_memory_space_constraint(x, pltpu.VMEM) for x in made))
    return tuple(out.reshape(vec_prev.shape) for out in outs)


def solution(mesh):
    fields = P(None, None, "gx", "gy", None)
    return jax.shard_map(
        shards,
        mesh=mesh,
        in_specs=(
            P(None, "gx", "gy", None),
            P("gx", "gy", None),
            P("gx", "gy", None),
            P("gx", "gy", None, None),
            fields,
            fields,
            fields,
            fields,
        ),
        out_specs=(fields,) * 4,
        check_vma=False,
    )
```

```python
import functools

import jax
import jax.numpy as jnp
from jax import lax
from jax.experimental import pallas as pl
from jax.experimental.pallas import tpu as pltpu
from jax.sharding import PartitionSpec as P

column_edge = 20.0
reach_sq = 64.0
MESH = pl.DeviceIdType.MESH
offsets = (0, 1, 2, 3, 5, 6, 7, 8)
departures = (5, 6, 7, 2, 3, 4, 0, 1)
arrivals = ((1, 6, 2, 4, 7, 0, 3, 5), (1, 6, 0, 3, 5, 2, 4, 7))
pairs = ((0, 0), (0, 1), (1, 1), (1, 2), (2, 2), (0, 2))


def halves(values):
    high = values.astype(jnp.bfloat16)
    return high, (values - high.astype(jnp.float32)).astype(jnp.bfloat16)


def kernel(
    count_x, count_y,
    pos_hbm, spring_hbm, border_hbm, nbr_hbm, vp_hbm, vn_hbm, hp_hbm, hn_hbm,
    vec_next, vec_after, heat_next, heat_after,
    geo_buf, border_ref, nbr_ref, field_buf, out_buf, in_buf, key_buf, amount_buf, times_buf,
    mat_buf, load_sem, send_sem, recv_sem,
):
    n_slots, n_atoms = nbr_ref.shape
    n_border = border_ref.shape[1]
    groups = n_atoms // n_border
    n_vec = field_buf.shape[1] // 3
    n_rows = 2 * n_vec
    gx, gy = lax.axis_index("gx"), lax.axis_index("gy")

    def device(rank):
        dx, dy = offsets[rank] // 3 - 1, offsets[rank] % 3 - 1
        return lax.rem(gx + dx + count_x, count_x), lax.rem(gy + dy + count_y, count_y)

    def either(low, one, other):
        return one if isinstance(one, int) and one == other else jnp.where(low, one, other)

    lower = 2 * gy < count_y
    places = [
        either(2 * device(rank)[1] < count_y, *(order.index(7 - rank) for order in arrivals))
        for rank in range(8)
    ]
    targets = []
    for turn in departures:
        one, other = (order[turn] for order in arrivals)
        if one == other:
            targets.append((device(one), places[one]))
        else:
            targets.append((
                tuple(jnp.where(lower, x, y) for x, y in zip(device(one), device(other))),
                jnp.where(lower, places[one], places[other]),
            ))

    barrier = pltpu.get_barrier_semaphore()
    for target, _ in targets:
        pl.semaphore_signal(barrier, inc=1, device_id=target, device_id_type=MESH)

    geo_buf[...] = jnp.zeros_like(geo_buf)
    moves = (
        (border_hbm, border_ref),
        (vn_hbm, field_buf.at[0]),
        (hn_hbm, field_buf.at[1]),
        (pos_hbm.at[0], geo_buf.at[0:1]),
        (pos_hbm.at[1], geo_buf.at[1:2]),
        (pos_hbm.at[2], geo_buf.at[2:3]),
        (spring_hbm, geo_buf.at[3:4]),
        (nbr_hbm, nbr_ref),
        (vp_hbm, field_buf.at[2]),
        (hp_hbm, field_buf.at[3]),
    )
    loads = [
        pltpu.make_async_copy(src, dst, load_sem.at[i]) for i, (src, dst) in enumerate(moves)
    ]
    for load in loads:
        load.start()
    for load in loads[:7]:
        load.wait()

    lane_group = lax.broadcasted_iota(jnp.int32, (n_rows, n_atoms), 1) // n_border
    chosen = jnp.concatenate([border_ref[...]] * groups, axis=1)
    chosen = jnp.broadcast_to(chosen, (n_rows, n_atoms))

    def copies(turn):
        return [
            pltpu.make_async_remote_copy(
                src_ref=out_buf.at[turn, place % 4],
                dst_ref=in_buf.at[turn, place],
                send_sem=send_sem.at[turn, index],
                recv_sem=recv_sem.at[turn, place],
                device_id=target,
                device_id_type=MESH,
            )
            for index, (target, place) in enumerate(targets)
        ]

    def arrive(turn, first, last):
        for place in range(first, last):
            pltpu.make_async_remote_copy(
                src_ref=out_buf.at[turn, 0],
                dst_ref=in_buf.at[turn, place],
                send_sem=send_sem.at[turn, 0],
                recv_sem=recv_sem.at[turn, place],
                device_id=device(0),
                device_id_type=MESH,
            ).wait_recv()

    def pack(turn, parts):
        taken = [jnp.take_along_axis(part, chosen, axis=1) for part in parts]
        for k in range(4):
            mixed = taken[0]
            for s in range(1, len(taken)):
                mixed = jnp.where(lane_group == (s + k) % 4, taken[s], mixed)
            out_buf[turn, k] = mixed

    def unpack(turn, half):
        tiles = []
        for s in range(3):
            mixed = in_buf[turn, 4 * half + (0 - s) % 4]
            for g in range(1, 4):
                mixed = jnp.where(lane_group == g, in_buf[turn, 4 * half + (g - s) % 4], mixed)
            tiles.append(pltpu.roll(mixed, (n_atoms - n_border * s) % n_atoms, 1) if s else mixed)
        return tiles

    def fields(vec, heat):
        return [
            jnp.concatenate(
                [vec[a * n_vec : (a + 1) * n_vec], heat[a * n_vec : (a + 1) * n_vec]], axis=0
            )
            for a in range(3)
        ]

    geometry = geo_buf[...]
    row_of = lax.broadcasted_iota(jnp.int32, geometry.shape, 0)
    geometry = jnp.where(row_of == 3, jnp.sqrt(geometry), geometry)
    own_pos = geometry[0:3]
    root = geometry[3:4]
    state_one = fields(field_buf[0], field_buf[1])
    pack(0, state_one + [geometry])

    loads[7].wait()
    entries = nbr_ref[...]
    shift = n_atoms.bit_length() - 1
    small = n_border.bit_length() - 1
    offset = entries >> shift
    within = entries & (n_atoms - 1)
    block = jnp.where(
        offset == 4, within >> small, jnp.where(offset > 4, offset + groups - 1, offset + groups)
    )
    word = (block >> 2) * n_border + (within & (n_border - 1))
    key_buf[...] = jnp.where(entries < 0, -1, word)
    amount_buf[...] = jnp.left_shift(jnp.int32(1), (block & 3) * 8)
    n_words = 3 * n_border
    numbers = lax.broadcasted_iota(jnp.int32, (n_words, n_atoms), 0)

    def add_slots(turn, total):
        start = pl.multiple_of(turn * 8, 8)
        keys = key_buf[pl.ds(start, 8), :]
        amounts = amount_buf[pl.ds(start, 8), :]
        for n in range(8):
            total = total + jnp.where(numbers == keys[n : n + 1], amounts[n : n + 1], 0)
        return total

    words = lax.fori_loop(
        0, n_slots // 8, add_slots, jnp.zeros((n_words, n_atoms), jnp.int32)
    )
    for g in range(3):
        for f in range(4):
            row = (4 * g + f) * n_border
            part = words[g * n_border : (g + 1) * n_border]
            times_buf[row : row + n_border] = ((part >> (8 * f)) & 255).astype(jnp.float32)

    pl.semaphore_wait(barrier, 8)
    first = copies(0)
    for copy in first:
        copy.start()

    def slots_of(turn):
        start = turn * n_border
        return pl.ds(start if isinstance(turn, int) else pl.multiple_of(start, n_border), n_border)

    def build(turn, counts, columns, sums):
        tile, row = turn // groups, turn % groups * n_border
        delta = [columns[:, a : a + 1] - own_pos[a : a + 1] for a in range(3)]
        dist_sq = delta[0] * delta[0] + delta[1] * delta[1] + delta[2] * delta[2]
        scale = times_buf[counts, :] * (columns[:, 3:4] * root)
        near = dist_sq + 1.0
        share = scale / (near * (n_slots + dist_sq * (n_slots / reach_sq)))
        coupling = share * near
        bent = [(share + share) * part for part in delta]
        out = []
        for index, (a, b) in enumerate(pairs):
            entry = bent[a] * delta[b]
            if a == b:
                entry = entry + coupling
            high, low = halves(entry)
            lanes = slice(index * n_atoms, (index + 1) * n_atoms)
            mat_buf[tile, row : row + n_border, lanes] = high
            mat_buf[tile, n_atoms + row : n_atoms + row + n_border, lanes] = low
            out.append(sums[index] + jnp.sum(entry.reshape(-1, 8, n_atoms), axis=0))
        return tuple(out)

    def product(tile, sources):
        high, low = halves(jnp.concatenate(sources, axis=0))
        both = jnp.concatenate([high, low], axis=0)
        both = jnp.concatenate([both, both], axis=1)
        full = jnp.dot(both, mat_buf[tile], preferred_element_type=jnp.float32)
        return full[: 3 * n_rows] + full[3 * n_rows :]

    def pieces(full):
        return [
            [
                full[b * n_rows : (b + 1) * n_rows, index * n_atoms : (index + 1) * n_atoms]
                for index in range(6)
            ]
            for b in range(3)
        ]

    def gathered(full):
        part = pieces(full)
        place = {pair: index for index, pair in enumerate(pairs)}
        return [
            sum(part[b][place[(min(a, b), max(a, b))]] for b in range(3)) for a in range(3)
        ]

    sums = tuple(jnp.zeros((8, n_atoms), jnp.float32) for _ in pairs)
    columns = jnp.transpose(geometry[:8])
    for turn in range(groups):
        own = columns[turn * n_border : (turn + 1) * n_border]
        sums = build(turn, slots_of(turn), own, sums)
    total = product(0, state_one)

    component = lax.broadcasted_iota(jnp.int32, (1, 8), 1)

    def receive(first, last, sums):
        arrive(0, first, last)
        turned = [jnp.transpose(in_buf[0, place, :8, :]) for place in range(first, last)]
        for place in range(first, last):
            rank = either(lower, *(order[place] for order in arrivals))
            offset = rank + jnp.where(jnp.int32(rank) >= 4, 1, 0)
            step_x = offset // 3 - 1
            step_y = offset - 3 * (step_x + 1) - 1
            step = jnp.where(component == 0, step_x, jnp.where(component == 1, step_y, 0))
            start = (place + 3) % 4 * n_border
            columns = turned[place - first][start : start + n_border]
            columns = columns + step.astype(jnp.float32) * column_edge
            sums = build(groups + place, slots_of(groups + rank), columns, sums)
        return sums

    sums = receive(0, 5, sums)
    total = total + product(1, unpack(0, 0))
    sums = receive(5, 8, sums)
    totals = [jnp.sum(part, axis=0, keepdims=True) for part in sums]
    weight = {pair: total for pair, total in zip(pairs, totals)}

    def stepped(state, before, far):
        out = []
        for a in range(3):
            value = sum(weight[(min(a, b), max(a, b))] * state[b] for b in range(3))
            out.append(2.0 * (value - far[a] - state[a]) - before[a])
        return out

    far = gathered(total + product(2, unpack(0, 1)))
    for load in loads[8:]:
        load.wait()
    state_two = stepped(state_one, fields(field_buf[2], field_buf[3]), far)
    pack(1, state_two)
    second = copies(1)
    for copy in second:
        copy.start()
    for a in range(3):
        vec_next[a * n_vec : (a + 1) * n_vec] = state_two[a][:n_vec]
        heat_next[a * n_vec : (a + 1) * n_vec] = state_two[a][n_vec:]
    total = product(0, state_two)
    arrive(1, 0, 4)
    total = total + product(1, unpack(1, 0))
    arrive(1, 4, 8)
    far = gathered(total + product(2, unpack(1, 1)))
    state_three = stepped(state_two, state_one, far)
    for a in range(3):
        vec_after[a * n_vec : (a + 1) * n_vec] = state_three[a][:n_vec]
        heat_after[a * n_vec : (a + 1) * n_vec] = state_three[a][n_vec:]
    for copy in first + second:
        copy.wait_send()


def deliver(*refs):
    sem = refs[8]
    moves = [pltpu.make_async_copy(refs[i], refs[4 + i], sem.at[i]) for i in range(4)]
    for move in moves:
        move.start()
    for move in moves:
        move.wait()


def shards(positions, spring, border, neighbours, vec_prev, vec_now, heat_prev, heat_now):
    n_atoms = spring.shape[-1]
    n_slots = neighbours.shape[2]
    n_border = border.shape[-1]
    n_vec = vec_prev.shape[1]
    n_rows = 2 * n_vec
    flat = jax.ShapeDtypeStruct((3 * n_vec, n_atoms), jnp.float32)
    vmem = pl.BlockSpec(memory_space=pltpu.VMEM)
    hbm = pl.BlockSpec(memory_space=pltpu.HBM)
    made = pl.pallas_call(
        functools.partial(kernel, lax.axis_size("gx"), lax.axis_size("gy")),
        out_shape=(pltpu.VMEM(flat.shape, flat.dtype),) * 4,
        in_specs=[hbm] * 8,
        out_specs=(vmem,) * 4,
        scratch_shapes=[
            pltpu.VMEM((n_rows, n_atoms), jnp.float32),
            pltpu.VMEM((1, n_border), jnp.int32),
            pltpu.VMEM((n_slots, n_atoms), jnp.int32),
            pltpu.VMEM((4, 3 * n_vec, n_atoms), jnp.float32),
            pltpu.VMEM((2, 4, n_rows, n_atoms), jnp.float32),
            pltpu.VMEM((2, 8, n_rows, n_atoms), jnp.float32),
            pltpu.VMEM((n_slots, n_atoms), jnp.int32),
            pltpu.VMEM((n_slots, n_atoms), jnp.int32),
            pltpu.VMEM((3 * n_atoms, n_atoms), jnp.float32),
            pltpu.VMEM((3, 2 * n_atoms, 6 * n_atoms), jnp.bfloat16),
            pltpu.SemaphoreType.DMA((10,)),
            pltpu.SemaphoreType.DMA((2, 8)),
            pltpu.SemaphoreType.DMA((2, 8)),
        ],
        compiler_params=pltpu.CompilerParams(
            collective_id=0, has_side_effects=True, vmem_limit_bytes=24 * 1024 * 1024
        ),
        name="chebyshev",
    )(
        *(
            pltpu.with_memory_space_constraint(x, pltpu.HBM)
            for x in (
                positions.reshape(3, 1, n_atoms),
                spring.reshape(1, n_atoms),
                border.reshape(1, n_border),
                neighbours.reshape(n_slots, n_atoms),
                *(x.reshape(3 * n_vec, n_atoms) for x in (vec_prev, vec_now, heat_prev, heat_now)),
            )
        ),
    )
    outs = pl.pallas_call(
        deliver,
        out_shape=(flat,) * 4,
        in_specs=[vmem] * 4,
        out_specs=(hbm,) * 4,
        scratch_shapes=[pltpu.SemaphoreType.DMA((4,))],
        name="deliver",
    )(*(pltpu.with_memory_space_constraint(x, pltpu.VMEM) for x in made))
    return tuple(out.reshape(vec_prev.shape) for out in outs)


def solution(mesh):
    fields = P(None, None, "gx", "gy", None)
    return jax.shard_map(
        shards,
        mesh=mesh,
        in_specs=(
            P(None, "gx", "gy", None),
            P("gx", "gy", None),
            P("gx", "gy", None),
            P("gx", "gy", None, None),
            fields,
            fields,
            fields,
            fields,
        ),
        out_specs=(fields,) * 4,
        check_vma=False,
    )
```

```python
import functools

import jax
import jax.numpy as jnp
from jax import lax
from jax.experimental import pallas as pl
from jax.experimental.pallas import tpu as pltpu
from jax.sharding import PartitionSpec as P

column_edge = 20.0
reach_sq = 64.0
MESH = pl.DeviceIdType.MESH
offsets = (0, 1, 2, 3, 5, 6, 7, 8)
departures = (5, 6, 7, 2, 3, 4, 0, 1)
arrivals = ((1, 6, 2, 4, 7, 0, 3, 5), (1, 6, 0, 3, 5, 2, 4, 7))
pairs = ((0, 0), (0, 1), (1, 1), (1, 2), (2, 2), (0, 2))


def halves(values):
    high = values.astype(jnp.bfloat16)
    return high, (values - high.astype(jnp.float32)).astype(jnp.bfloat16)


def kernel(
    count_x, count_y,
    pos_hbm, spring_hbm, border_hbm, nbr_hbm, vp_hbm, vn_hbm, hp_hbm, hn_hbm,
    vec_next, vec_after, heat_next, heat_after,
    geo_buf, border_ref, nbr_ref, field_buf, out_buf, in_buf, key_buf, amount_buf, times_buf,
    mat_buf, load_sem, send_sem, recv_sem,
):
    n_slots, n_atoms = nbr_ref.shape
    n_border = border_ref.shape[1]
    groups = n_atoms // n_border
    n_vec = field_buf.shape[1] // 3
    n_rows = 2 * n_vec
    gx, gy = lax.axis_index("gx"), lax.axis_index("gy")

    def device(rank):
        dx, dy = offsets[rank] // 3 - 1, offsets[rank] % 3 - 1
        return lax.rem(gx + dx + count_x, count_x), lax.rem(gy + dy + count_y, count_y)

    def either(low, one, other):
        return one if isinstance(one, int) and one == other else jnp.where(low, one, other)

    lower = 2 * gy < count_y
    places = [
        either(2 * device(rank)[1] < count_y, *(order.index(7 - rank) for order in arrivals))
        for rank in range(8)
    ]
    targets = []
    for turn in departures:
        one, other = (order[turn] for order in arrivals)
        if one == other:
            targets.append((device(one), places[one]))
        else:
            targets.append((
                tuple(jnp.where(lower, x, y) for x, y in zip(device(one), device(other))),
                jnp.where(lower, places[one], places[other]),
            ))

    barrier = pltpu.get_barrier_semaphore()
    for target, _ in targets:
        pl.semaphore_signal(barrier, inc=1, device_id=target, device_id_type=MESH)

    geo_buf[...] = jnp.zeros_like(geo_buf)
    moves = (
        (border_hbm, border_ref),
        (vn_hbm, field_buf.at[0]),
        (hn_hbm, field_buf.at[1]),
        (pos_hbm.at[0], geo_buf.at[0:1]),
        (pos_hbm.at[1], geo_buf.at[1:2]),
        (pos_hbm.at[2], geo_buf.at[2:3]),
        (spring_hbm, geo_buf.at[3:4]),
        (nbr_hbm, nbr_ref),
        (vp_hbm, field_buf.at[2]),
        (hp_hbm, field_buf.at[3]),
    )
    loads = [
        pltpu.make_async_copy(src, dst, load_sem.at[i]) for i, (src, dst) in enumerate(moves)
    ]
    for load in loads:
        load.start()
    for load in loads[:7]:
        load.wait()

    lane_group = lax.broadcasted_iota(jnp.int32, (n_rows, n_atoms), 1) // n_border
    chosen = jnp.concatenate([border_ref[...]] * groups, axis=1)
    chosen = jnp.broadcast_to(chosen, (n_rows, n_atoms))

    def copies(turn):
        return [
            pltpu.make_async_remote_copy(
                src_ref=out_buf.at[turn, place % 4],
                dst_ref=in_buf.at[turn, place],
                send_sem=send_sem.at[turn, index],
                recv_sem=recv_sem.at[turn, place],
                device_id=target,
                device_id_type=MESH,
            )
            for index, (target, place) in enumerate(targets)
        ]

    def arrive(turn, first, last):
        for place in range(first, last):
            pltpu.make_async_remote_copy(
                src_ref=out_buf.at[turn, 0],
                dst_ref=in_buf.at[turn, place],
                send_sem=send_sem.at[turn, 0],
                recv_sem=recv_sem.at[turn, place],
                device_id=device(0),
                device_id_type=MESH,
            ).wait_recv()

    def pack(turn, parts):
        taken = [jnp.take_along_axis(part, chosen, axis=1) for part in parts]
        for k in range(4):
            mixed = taken[0]
            for s in range(1, len(taken)):
                mixed = jnp.where(lane_group == (s + k) % 4, taken[s], mixed)
            out_buf[turn, k] = mixed

    def unpack(turn, half):
        tiles = []
        for s in range(3):
            mixed = in_buf[turn, 4 * half + (0 - s) % 4]
            for g in range(1, 4):
                mixed = jnp.where(lane_group == g, in_buf[turn, 4 * half + (g - s) % 4], mixed)
            tiles.append(pltpu.roll(mixed, (n_atoms - n_border * s) % n_atoms, 1) if s else mixed)
        return tiles

    def fields(vec, heat):
        return [
            jnp.concatenate(
                [vec[a * n_vec : (a + 1) * n_vec], heat[a * n_vec : (a + 1) * n_vec]], axis=0
            )
            for a in range(3)
        ]

    geometry = geo_buf[...]
    row_of = lax.broadcasted_iota(jnp.int32, geometry.shape, 0)
    geometry = jnp.where(row_of == 3, jnp.sqrt(geometry), geometry)
    own_pos = geometry[0:3]
    root = geometry[3:4]
    state_one = fields(field_buf[0], field_buf[1])
    pack(0, state_one + [geometry])

    loads[7].wait()
    entries = nbr_ref[...]
    shift = n_atoms.bit_length() - 1
    small = n_border.bit_length() - 1
    offset = entries >> shift
    within = entries & (n_atoms - 1)
    block = jnp.where(
        offset == 4, within >> small, jnp.where(offset > 4, offset + groups - 1, offset + groups)
    )
    word = (block >> 2) * n_border + (within & (n_border - 1))
    key_buf[...] = jnp.where(entries < 0, -1, word)
    amount_buf[...] = jnp.left_shift(jnp.int32(1), (block & 3) * 8)
    n_words = 3 * n_border
    numbers = lax.broadcasted_iota(jnp.int32, (n_words, n_atoms), 0)

    def add_slots(turn, total):
        start = pl.multiple_of(turn * 8, 8)
        keys = key_buf[pl.ds(start, 8), :]
        amounts = amount_buf[pl.ds(start, 8), :]
        for n in range(8):
            total = total + jnp.where(numbers == keys[n : n + 1], amounts[n : n + 1], 0)
        return total

    words = lax.fori_loop(
        0, n_slots // 8, add_slots, jnp.zeros((n_words, n_atoms), jnp.int32)
    )
    for g in range(3):
        for f in range(4):
            row = (4 * g + f) * n_border
            part = words[g * n_border : (g + 1) * n_border]
            times_buf[row : row + n_border] = ((part >> (8 * f)) & 255).astype(jnp.float32)

    pl.semaphore_wait(barrier, 8)
    first = copies(0)
    for copy in first:
        copy.start()

    picked = lax.broadcasted_iota(jnp.int32, (24, 4 * n_atoms), 0) % 8
    lane_part = lax.broadcasted_iota(jnp.int32, (24, 4 * n_atoms), 1) // n_atoms
    selector = (picked == lane_part).astype(jnp.float32).astype(jnp.bfloat16)

    def turned(rows):
        high = rows.astype(jnp.bfloat16).astype(jnp.float32)
        middle = (rows - high).astype(jnp.bfloat16).astype(jnp.float32)
        parts = jnp.concatenate([high, middle, rows - high - middle], axis=0)
        return jnp.transpose(parts).astype(jnp.bfloat16)

    def slots_of(turn):
        start = turn * n_border
        return pl.ds(start if isinstance(turn, int) else pl.multiple_of(start, n_border), n_border)

    def build(turn, counts, columns, sums):
        tile, row = turn // groups, turn % groups * n_border
        spread = jnp.dot(columns, selector, preferred_element_type=jnp.float32)
        wide = [spread[:, a * n_atoms : (a + 1) * n_atoms] for a in range(4)]
        delta = [wide[a] - own_pos[a : a + 1] for a in range(3)]
        dist_sq = delta[0] * delta[0] + delta[1] * delta[1] + delta[2] * delta[2]
        scale = times_buf[counts, :] * (wide[3] * root)
        near = dist_sq + 1.0
        share = scale / (near * (n_slots + dist_sq * (n_slots / reach_sq)))
        coupling = share * near
        bent = [(share + share) * part for part in delta]
        out = []
        for index, (a, b) in enumerate(pairs):
            entry = bent[a] * delta[b]
            if a == b:
                entry = entry + coupling
            high, low = halves(entry)
            lanes = slice(index * n_atoms, (index + 1) * n_atoms)
            mat_buf[tile, row : row + n_border, lanes] = high
            mat_buf[tile, n_atoms + row : n_atoms + row + n_border, lanes] = low
            out.append(sums[index] + jnp.sum(entry.reshape(-1, 8, n_atoms), axis=0))
        return tuple(out)

    def product(tile, sources):
        high, low = halves(jnp.concatenate(sources, axis=0))
        both = jnp.concatenate([high, low], axis=0)
        both = jnp.concatenate([both, both], axis=1)
        full = jnp.dot(both, mat_buf[tile], preferred_element_type=jnp.float32)
        return full[: 3 * n_rows] + full[3 * n_rows :]

    def pieces(full):
        return [
            [
                full[b * n_rows : (b + 1) * n_rows, index * n_atoms : (index + 1) * n_atoms]
                for index in range(6)
            ]
            for b in range(3)
        ]

    def gathered(full):
        part = pieces(full)
        place = {pair: index for index, pair in enumerate(pairs)}
        return [
            sum(part[b][place[(min(a, b), max(a, b))]] for b in range(3)) for a in range(3)
        ]

    sums = tuple(jnp.zeros((8, n_atoms), jnp.float32) for _ in pairs)
    columns = turned(geometry[:8])
    for turn in range(groups):
        own = columns[turn * n_border : (turn + 1) * n_border]
        sums = build(turn, slots_of(turn), own, sums)
    total = product(0, state_one)

    component = lax.broadcasted_iota(jnp.int32, (8, n_atoms), 0)

    def receive(first, last, sums):
        arrive(0, first, last)
        for place in range(first, last):
            rank = either(lower, *(order[place] for order in arrivals))
            offset = rank + jnp.where(jnp.int32(rank) >= 4, 1, 0)
            step_x = offset // 3 - 1
            step_y = offset - 3 * (step_x + 1) - 1
            step = jnp.where(component == 0, step_x, jnp.where(component == 1, step_y, 0))
            start = (place + 3) % 4 * n_border
            rows = in_buf[0, place, :8, :] + step.astype(jnp.float32) * column_edge
            columns = turned(rows)[start : start + n_border]
            sums = build(groups + place, slots_of(groups + rank), columns, sums)
        return sums

    sums = receive(0, 5, sums)
    total = total + product(1, unpack(0, 0))
    sums = receive(5, 8, sums)
    totals = [jnp.sum(part, axis=0, keepdims=True) for part in sums]
    weight = {pair: total for pair, total in zip(pairs, totals)}

    def stepped(state, before, far):
        out = []
        for a in range(3):
            value = sum(weight[(min(a, b), max(a, b))] * state[b] for b in range(3))
            out.append(2.0 * (value - far[a] - state[a]) - before[a])
        return out

    far = gathered(total + product(2, unpack(0, 1)))
    for load in loads[8:]:
        load.wait()
    state_two = stepped(state_one, fields(field_buf[2], field_buf[3]), far)
    pack(1, state_two)
    second = copies(1)
    for copy in second:
        copy.start()
    for a in range(3):
        vec_next[a * n_vec : (a + 1) * n_vec] = state_two[a][:n_vec]
        heat_next[a * n_vec : (a + 1) * n_vec] = state_two[a][n_vec:]
    total = product(0, state_two)
    arrive(1, 0, 4)
    total = total + product(1, unpack(1, 0))
    arrive(1, 4, 8)
    far = gathered(total + product(2, unpack(1, 1)))
    state_three = stepped(state_two, state_one, far)
    for a in range(3):
        vec_after[a * n_vec : (a + 1) * n_vec] = state_three[a][:n_vec]
        heat_after[a * n_vec : (a + 1) * n_vec] = state_three[a][n_vec:]
    for copy in first + second:
        copy.wait_send()


def deliver(*refs):
    sem = refs[8]
    moves = [pltpu.make_async_copy(refs[i], refs[4 + i], sem.at[i]) for i in range(4)]
    for move in moves:
        move.start()
    for move in moves:
        move.wait()


def shards(positions, spring, border, neighbours, vec_prev, vec_now, heat_prev, heat_now):
    n_atoms = spring.shape[-1]
    n_slots = neighbours.shape[2]
    n_border = border.shape[-1]
    n_vec = vec_prev.shape[1]
    n_rows = 2 * n_vec
    flat = jax.ShapeDtypeStruct((3 * n_vec, n_atoms), jnp.float32)
    vmem = pl.BlockSpec(memory_space=pltpu.VMEM)
    hbm = pl.BlockSpec(memory_space=pltpu.HBM)
    made = pl.pallas_call(
        functools.partial(kernel, lax.axis_size("gx"), lax.axis_size("gy")),
        out_shape=(pltpu.VMEM(flat.shape, flat.dtype),) * 4,
        in_specs=[hbm] * 8,
        out_specs=(vmem,) * 4,
        scratch_shapes=[
            pltpu.VMEM((n_rows, n_atoms), jnp.float32),
            pltpu.VMEM((1, n_border), jnp.int32),
            pltpu.VMEM((n_slots, n_atoms), jnp.int32),
            pltpu.VMEM((4, 3 * n_vec, n_atoms), jnp.float32),
            pltpu.VMEM((2, 4, n_rows, n_atoms), jnp.float32),
            pltpu.VMEM((2, 8, n_rows, n_atoms), jnp.float32),
            pltpu.VMEM((n_slots, n_atoms), jnp.int32),
            pltpu.VMEM((n_slots, n_atoms), jnp.int32),
            pltpu.VMEM((3 * n_atoms, n_atoms), jnp.float32),
            pltpu.VMEM((3, 2 * n_atoms, 6 * n_atoms), jnp.bfloat16),
            pltpu.SemaphoreType.DMA((10,)),
            pltpu.SemaphoreType.DMA((2, 8)),
            pltpu.SemaphoreType.DMA((2, 8)),
        ],
        compiler_params=pltpu.CompilerParams(
            collective_id=0, has_side_effects=True, vmem_limit_bytes=24 * 1024 * 1024
        ),
        name="chebyshev",
    )(
        *(
            pltpu.with_memory_space_constraint(x, pltpu.HBM)
            for x in (
                positions.reshape(3, 1, n_atoms),
                spring.reshape(1, n_atoms),
                border.reshape(1, n_border),
                neighbours.reshape(n_slots, n_atoms),
                *(x.reshape(3 * n_vec, n_atoms) for x in (vec_prev, vec_now, heat_prev, heat_now)),
            )
        ),
    )
    outs = pl.pallas_call(
        deliver,
        out_shape=(flat,) * 4,
        in_specs=[vmem] * 4,
        out_specs=(hbm,) * 4,
        scratch_shapes=[pltpu.SemaphoreType.DMA((4,))],
        name="deliver",
    )(*(pltpu.with_memory_space_constraint(x, pltpu.VMEM) for x in made))
    return tuple(out.reshape(vec_prev.shape) for out in outs)


def solution(mesh):
    fields = P(None, None, "gx", "gy", None)
    return jax.shard_map(
        shards,
        mesh=mesh,
        in_specs=(
            P(None, "gx", "gy", None),
            P("gx", "gy", None),
            P("gx", "gy", None),
            P("gx", "gy", None, None),
            fields,
            fields,
            fields,
            fields,
        ),
        out_specs=(fields,) * 4,
        check_vma=False,
    )
```

```python
import functools

import jax
import jax.numpy as jnp
from jax import lax
from jax.experimental import pallas as pl
from jax.experimental.pallas import tpu as pltpu
from jax.sharding import PartitionSpec as P

column_edge = 20.0
reach_sq = 64.0
MESH = pl.DeviceIdType.MESH
offsets = (0, 1, 2, 3, 5, 6, 7, 8)
departures = (5, 6, 7, 2, 3, 4, 0, 1)
arrivals = ((1, 6, 2, 4, 7, 0, 3, 5), (1, 6, 0, 3, 5, 2, 4, 7))
pairs = ((0, 0), (0, 1), (1, 1), (1, 2), (2, 2), (0, 2))


def halves(values):
    high = values.astype(jnp.bfloat16)
    return high, (values - high.astype(jnp.float32)).astype(jnp.bfloat16)


def kernel(
    count_x, count_y,
    pos_hbm, spring_hbm, border_hbm, nbr_hbm, vp_hbm, vn_hbm, hp_hbm, hn_hbm,
    vec_next, vec_after, heat_next, heat_after,
    geo_buf, border_ref, nbr_ref, field_buf, out_buf, in_buf, key_buf, amount_buf, times_buf,
    mat_buf, load_sem, send_sem, recv_sem,
):
    n_slots, n_atoms = nbr_ref.shape
    n_border = border_ref.shape[1]
    groups = n_atoms // n_border
    n_vec = field_buf.shape[1] // 3
    n_rows = 2 * n_vec
    gx, gy = lax.axis_index("gx"), lax.axis_index("gy")

    def device(rank):
        dx, dy = offsets[rank] // 3 - 1, offsets[rank] % 3 - 1
        return lax.rem(gx + dx + count_x, count_x), lax.rem(gy + dy + count_y, count_y)

    def either(low, one, other):
        return one if isinstance(one, int) and one == other else jnp.where(low, one, other)

    lower = 2 * gy < count_y
    places = [
        either(2 * device(rank)[1] < count_y, *(order.index(7 - rank) for order in arrivals))
        for rank in range(8)
    ]
    targets = []
    for turn in departures:
        one, other = (order[turn] for order in arrivals)
        if one == other:
            targets.append((device(one), places[one]))
        else:
            targets.append((
                tuple(jnp.where(lower, x, y) for x, y in zip(device(one), device(other))),
                jnp.where(lower, places[one], places[other]),
            ))

    barrier = pltpu.get_barrier_semaphore()
    for target, _ in targets:
        pl.semaphore_signal(barrier, inc=1, device_id=target, device_id_type=MESH)

    geo_buf[...] = jnp.zeros_like(geo_buf)
    moves = (
        (border_hbm, border_ref),
        (vn_hbm, field_buf.at[0]),
        (hn_hbm, field_buf.at[1]),
        (pos_hbm.at[0], geo_buf.at[0:1]),
        (pos_hbm.at[1], geo_buf.at[1:2]),
        (pos_hbm.at[2], geo_buf.at[2:3]),
        (spring_hbm, geo_buf.at[3:4]),
        (nbr_hbm, nbr_ref),
        (vp_hbm, field_buf.at[2]),
        (hp_hbm, field_buf.at[3]),
    )
    loads = [
        pltpu.make_async_copy(src, dst, load_sem.at[i]) for i, (src, dst) in enumerate(moves)
    ]
    for load in loads:
        load.start()
    for load in loads[:7]:
        load.wait()

    lane_group = lax.broadcasted_iota(jnp.int32, (n_rows, n_atoms), 1) // n_border
    chosen = jnp.concatenate([border_ref[...]] * groups, axis=1)
    chosen = jnp.broadcast_to(chosen, (n_rows, n_atoms))

    def copies(turn):
        return [
            pltpu.make_async_remote_copy(
                src_ref=out_buf.at[turn, place % 4],
                dst_ref=in_buf.at[turn, place],
                send_sem=send_sem.at[turn, index],
                recv_sem=recv_sem.at[turn, place],
                device_id=target,
                device_id_type=MESH,
            )
            for index, (target, place) in enumerate(targets)
        ]

    def arrive(turn, first, last):
        for place in range(first, last):
            pltpu.make_async_remote_copy(
                src_ref=out_buf.at[turn, 0],
                dst_ref=in_buf.at[turn, place],
                send_sem=send_sem.at[turn, 0],
                recv_sem=recv_sem.at[turn, place],
                device_id=device(0),
                device_id_type=MESH,
            ).wait_recv()

    def pack(turn, parts):
        taken = [jnp.take_along_axis(part, chosen, axis=1) for part in parts]
        for k in range(4):
            mixed = taken[0]
            for s in range(1, len(taken)):
                mixed = jnp.where(lane_group == (s + k) % 4, taken[s], mixed)
            out_buf[turn, k] = mixed

    def unpack(turn, half):
        tiles = []
        for s in range(3):
            mixed = in_buf[turn, 4 * half + (0 - s) % 4]
            for g in range(1, 4):
                mixed = jnp.where(lane_group == g, in_buf[turn, 4 * half + (g - s) % 4], mixed)
            tiles.append(pltpu.roll(mixed, (n_atoms - n_border * s) % n_atoms, 1) if s else mixed)
        return tiles

    def fields(vec, heat):
        return [
            jnp.concatenate(
                [vec[a * n_vec : (a + 1) * n_vec], heat[a * n_vec : (a + 1) * n_vec]], axis=0
            )
            for a in range(3)
        ]

    geometry = geo_buf[...]
    row_of = lax.broadcasted_iota(jnp.int32, geometry.shape, 0)
    geometry = jnp.where(row_of == 3, jnp.sqrt(geometry), geometry)
    own_pos = geometry[0:3]
    root = geometry[3:4]
    state_one = fields(field_buf[0], field_buf[1])
    pack(0, state_one + [geometry])

    pl.semaphore_wait(barrier, 8)
    first = copies(0)
    for copy in first:
        copy.start()

    loads[7].wait()
    entries = nbr_ref[...]
    shift = n_atoms.bit_length() - 1
    small = n_border.bit_length() - 1
    offset = entries >> shift
    within = entries & (n_atoms - 1)
    block = jnp.where(
        offset == 4, within >> small, jnp.where(offset > 4, offset + groups - 1, offset + groups)
    )
    word = (block >> 2) * n_border + (within & (n_border - 1))
    key_buf[...] = jnp.where(entries < 0, -1, word)
    amount_buf[...] = jnp.left_shift(jnp.int32(1), (block & 3) * 8)
    n_words = 3 * n_border
    numbers = lax.broadcasted_iota(jnp.int32, (n_words, n_atoms), 0)

    def add_slots(turn, total):
        start = pl.multiple_of(turn * 8, 8)
        keys = key_buf[pl.ds(start, 8), :]
        amounts = amount_buf[pl.ds(start, 8), :]
        for n in range(8):
            total = total + jnp.where(numbers == keys[n : n + 1], amounts[n : n + 1], 0)
        return total

    words = lax.fori_loop(
        0, n_slots // 8, add_slots, jnp.zeros((n_words, n_atoms), jnp.int32)
    )
    for g in range(3):
        for f in range(4):
            row = (4 * g + f) * n_border
            part = words[g * n_border : (g + 1) * n_border]
            times_buf[row : row + n_border] = ((part >> (8 * f)) & 255).astype(jnp.float32)

    picked = lax.broadcasted_iota(jnp.int32, (24, 4 * n_atoms), 0) % 8
    lane_part = lax.broadcasted_iota(jnp.int32, (24, 4 * n_atoms), 1) // n_atoms
    selector = (picked == lane_part).astype(jnp.float32).astype(jnp.bfloat16)

    def turned(rows):
        high = rows.astype(jnp.bfloat16).astype(jnp.float32)
        middle = (rows - high).astype(jnp.bfloat16).astype(jnp.float32)
        parts = jnp.concatenate([high, middle, rows - high - middle], axis=0)
        return jnp.transpose(parts).astype(jnp.bfloat16)

    def slots_of(turn):
        start = turn * n_border
        return pl.ds(start if isinstance(turn, int) else pl.multiple_of(start, n_border), n_border)

    def build(turn, counts, columns, sums):
        tile, row = turn // groups, turn % groups * n_border
        spread = jnp.dot(columns, selector, preferred_element_type=jnp.float32)
        wide = [spread[:, a * n_atoms : (a + 1) * n_atoms] for a in range(4)]
        delta = [wide[a] - own_pos[a : a + 1] for a in range(3)]
        dist_sq = delta[0] * delta[0] + delta[1] * delta[1] + delta[2] * delta[2]
        scale = times_buf[counts, :] * (wide[3] * root)
        near = dist_sq + 1.0
        share = scale / (near * (n_slots + dist_sq * (n_slots / reach_sq)))
        coupling = share * near
        bent = [(share + share) * part for part in delta]
        out = []
        for index, (a, b) in enumerate(pairs):
            entry = bent[a] * delta[b]
            if a == b:
                entry = entry + coupling
            high, low = halves(entry)
            lanes = slice(index * n_atoms, (index + 1) * n_atoms)
            mat_buf[tile, row : row + n_border, lanes] = high
            mat_buf[tile, n_atoms + row : n_atoms + row + n_border, lanes] = low
            out.append(sums[index] + jnp.sum(entry.reshape(-1, 8, n_atoms), axis=0))
        return tuple(out)

    def product(tile, sources):
        high, low = halves(jnp.concatenate(sources, axis=0))
        both = jnp.concatenate([high, low], axis=0)
        both = jnp.concatenate([both, both], axis=1)
        full = jnp.dot(both, mat_buf[tile], preferred_element_type=jnp.float32)
        return full[: 3 * n_rows] + full[3 * n_rows :]

    def pieces(full):
        return [
            [
                full[b * n_rows : (b + 1) * n_rows, index * n_atoms : (index + 1) * n_atoms]
                for index in range(6)
            ]
            for b in range(3)
        ]

    def gathered(full):
        part = pieces(full)
        place = {pair: index for index, pair in enumerate(pairs)}
        return [
            sum(part[b][place[(min(a, b), max(a, b))]] for b in range(3)) for a in range(3)
        ]

    sums = tuple(jnp.zeros((8, n_atoms), jnp.float32) for _ in pairs)
    columns = turned(geometry[:8])
    for turn in range(groups):
        own = columns[turn * n_border : (turn + 1) * n_border]
        sums = build(turn, slots_of(turn), own, sums)
    total = product(0, state_one)

    component = lax.broadcasted_iota(jnp.int32, (8, n_atoms), 0)

    def receive(first, last, sums):
        arrive(0, first, last)
        for place in range(first, last):
            rank = either(lower, *(order[place] for order in arrivals))
            offset = rank + jnp.where(jnp.int32(rank) >= 4, 1, 0)
            step_x = offset // 3 - 1
            step_y = offset - 3 * (step_x + 1) - 1
            step = jnp.where(component == 0, step_x, jnp.where(component == 1, step_y, 0))
            start = (place + 3) % 4 * n_border
            rows = in_buf[0, place, :8, :] + step.astype(jnp.float32) * column_edge
            columns = turned(rows)[start : start + n_border]
            sums = build(groups + place, slots_of(groups + rank), columns, sums)
        return sums

    sums = receive(0, 5, sums)
    total = total + product(1, unpack(0, 0))
    sums = receive(5, 8, sums)
    totals = [jnp.sum(part, axis=0, keepdims=True) for part in sums]
    weight = {pair: total for pair, total in zip(pairs, totals)}

    def stepped(state, before, far):
        out = []
        for a in range(3):
            value = sum(weight[(min(a, b), max(a, b))] * state[b] for b in range(3))
            out.append(2.0 * (value - far[a] - state[a]) - before[a])
        return out

    far = gathered(total + product(2, unpack(0, 1)))
    for load in loads[8:]:
        load.wait()
    state_two = stepped(state_one, fields(field_buf[2], field_buf[3]), far)
    pack(1, state_two)
    second = copies(1)
    for copy in second:
        copy.start()
    for a in range(3):
        vec_next[a * n_vec : (a + 1) * n_vec] = state_two[a][:n_vec]
        heat_next[a * n_vec : (a + 1) * n_vec] = state_two[a][n_vec:]
    total = product(0, state_two)
    arrive(1, 0, 4)
    total = total + product(1, unpack(1, 0))
    arrive(1, 4, 8)
    far = gathered(total + product(2, unpack(1, 1)))
    state_three = stepped(state_two, state_one, far)
    for a in range(3):
        vec_after[a * n_vec : (a + 1) * n_vec] = state_three[a][:n_vec]
        heat_after[a * n_vec : (a + 1) * n_vec] = state_three[a][n_vec:]
    for copy in first + second:
        copy.wait_send()


def deliver(*refs):
    sem = refs[8]
    moves = [pltpu.make_async_copy(refs[i], refs[4 + i], sem.at[i]) for i in range(4)]
    for move in moves:
        move.start()
    for move in moves:
        move.wait()


def shards(positions, spring, border, neighbours, vec_prev, vec_now, heat_prev, heat_now):
    n_atoms = spring.shape[-1]
    n_slots = neighbours.shape[2]
    n_border = border.shape[-1]
    n_vec = vec_prev.shape[1]
    n_rows = 2 * n_vec
    flat = jax.ShapeDtypeStruct((3 * n_vec, n_atoms), jnp.float32)
    vmem = pl.BlockSpec(memory_space=pltpu.VMEM)
    hbm = pl.BlockSpec(memory_space=pltpu.HBM)
    made = pl.pallas_call(
        functools.partial(kernel, lax.axis_size("gx"), lax.axis_size("gy")),
        out_shape=(pltpu.VMEM(flat.shape, flat.dtype),) * 4,
        in_specs=[hbm] * 8,
        out_specs=(vmem,) * 4,
        scratch_shapes=[
            pltpu.VMEM((n_rows, n_atoms), jnp.float32),
            pltpu.VMEM((1, n_border), jnp.int32),
            pltpu.VMEM((n_slots, n_atoms), jnp.int32),
            pltpu.VMEM((4, 3 * n_vec, n_atoms), jnp.float32),
            pltpu.VMEM((2, 4, n_rows, n_atoms), jnp.float32),
            pltpu.VMEM((2, 8, n_rows, n_atoms), jnp.float32),
            pltpu.VMEM((n_slots, n_atoms), jnp.int32),
            pltpu.VMEM((n_slots, n_atoms), jnp.int32),
            pltpu.VMEM((3 * n_atoms, n_atoms), jnp.float32),
            pltpu.VMEM((3, 2 * n_atoms, 6 * n_atoms), jnp.bfloat16),
            pltpu.SemaphoreType.DMA((10,)),
            pltpu.SemaphoreType.DMA((2, 8)),
            pltpu.SemaphoreType.DMA((2, 8)),
        ],
        compiler_params=pltpu.CompilerParams(
            collective_id=0, has_side_effects=True, vmem_limit_bytes=24 * 1024 * 1024
        ),
        name="chebyshev",
    )(
        *(
            pltpu.with_memory_space_constraint(x, pltpu.HBM)
            for x in (
                positions.reshape(3, 1, n_atoms),
                spring.reshape(1, n_atoms),
                border.reshape(1, n_border),
                neighbours.reshape(n_slots, n_atoms),
                *(x.reshape(3 * n_vec, n_atoms) for x in (vec_prev, vec_now, heat_prev, heat_now)),
            )
        ),
    )
    outs = pl.pallas_call(
        deliver,
        out_shape=(flat,) * 4,
        in_specs=[vmem] * 4,
        out_specs=(hbm,) * 4,
        scratch_shapes=[pltpu.SemaphoreType.DMA((4,))],
        name="deliver",
    )(*(pltpu.with_memory_space_constraint(x, pltpu.VMEM) for x in made))
    return tuple(out.reshape(vec_prev.shape) for out in outs)


def solution(mesh):
    fields = P(None, None, "gx", "gy", None)
    return jax.shard_map(
        shards,
        mesh=mesh,
        in_specs=(
            P(None, "gx", "gy", None),
            P("gx", "gy", None),
            P("gx", "gy", None),
            P("gx", "gy", None, None),
            fields,
            fields,
            fields,
            fields,
        ),
        out_specs=(fields,) * 4,
        check_vma=False,
    )
```
